32 devices in a mesh: sub: 8 (over y, x, core), slab: 4 (over z).
Axes of the slice: x: 2, y: 2, z: 4, core: 2. Of those that a mesh axis runs over, the one named last changes fastest.
Arguments:
- coarse_basis: bfloat16 [32, 32, 4000], P('sub', 'slab'), may hold values from -6 to 6
- jacobians: bfloat16 [4, 750, 750], replicated, may hold values from -0.21875 to 0.21875
- element_faces: int32 [640, 6], P(('sub', 'slab')), may hold values from 1 to 58, as said below
- element_type: int32 [640], P(('sub', 'slab')), may hold values from 0 to 3
- element_count: int32 [32], P(('sub', 'slab')), may hold values from 1 to 20, 480 in all
- vertex_ids: int32 [32, 32], P(('sub', 'slab')), may hold values from 0 to 31, as said below
Outputs:
- second_image: bfloat16 [32, 32, 4000], P('sub', 'slab')
- coarse_matrix: float32 [32, 32], P('sub')
The draws below stay inside these ranges and needn't reach their ends.
Inputs may be any that keep to these rules, and one draw needn't show every extreme that they name: `element_faces`: each row names six different cells of the subdomain's extended face grid of (6) x (10) cells, numbered row-major, the own face blocks at rows 1 to 4 and columns 1 to 8; never one of the four corner cells. Each subdomain's live slots are its first element_count slots. `vertex_ids`: the 32 ids of one subdomain are different.
All inputs are finite; a program needn't handle non-finite values. No bound on the sum of `element_count` on one device may be relied on, other than what follows from the above.
Results may differ from the reference program's by a relative error of at most 0.0049.
Values may be sent and summed in bfloat16 or wider, within the bound.
A program may use at most 64 MiB of HBM per device.

```python
import math
import jax
import jax.numpy as jnp
import numpy as np
from jax import lax

FD = 125
C = 32
ED = 750
JT = 4
FX = 4
FY = 8
E_CAP = 20
SUBDOMAINS = 32
ELEMENTS = 640
NV = 32
NX = 32
NY = 32
N_SUB = 8
N_SLAB = 4


def draw_element_faces(key, part):
    cells = (FX + 2) * (FY + 2)
    cell = jnp.arange(cells, dtype=jnp.int32)
    grid_row = cell // (FY + 2)
    grid_col = cell % (FY + 2)
    corner = ((grid_row == 0) | (grid_row == FX + 1)) & ((grid_col == 0) | (grid_col == FY + 1))
    scores = jax.random.randint(key, (ELEMENTS, cells), 0, 1 << 20, dtype=jnp.int32) * cells + cell[None, :]
    scores = jnp.where(corner[None, :], -1, scores)
    unused, picked = lax.top_k(scores, 6)
    return picked.astype(jnp.int32)


def draw_vertex_ids(key, part):
    vertex = jnp.arange(NV, dtype=jnp.int32)
    scores = jax.random.randint(key, (SUBDOMAINS, NV), 0, 1 << 16, dtype=jnp.int32) * NV + vertex[None, :]
    unused, picked = lax.top_k(scores, C)
    return picked.astype(jnp.int32)


def set_ends(values, rng, low, top_value):
    place = [jax.random.randint(jax.random.fold_in(rng, axis), (), 0, length) for axis, length in enumerate(values.shape)]
    main_axis = values.shape.index(max(values.shape))
    neighbour = place[:main_axis] + [(place[main_axis] + 1) % values.shape[main_axis]] + place[main_axis + 1:]
    return values.at[tuple(place)].set(low).at[tuple(neighbour)].set(top_value)


def shard_levels(stream_key, shape, cuts, smallest, top_value):
    def one(axis_at, shards_of):
        draws = jax.random.uniform(jax.random.fold_in(jax.random.fold_in(stream_key, 6), axis_at), (shards_of,), jnp.float32, smallest / len(cuts), top_value / len(cuts))
        return jnp.repeat(jnp.exp(draws), shape[axis_at] // shards_of).reshape((-1,) + (1,) * (len(shape) - axis_at - 1))

    loudness = one(*cuts[0])
    for cut in cuts[1:]:
        loudness = loudness * one(*cut)
    return loudness


def split_up(count, total, most, lean):
    loads = [(1 << 20) // math.isqrt(grade ** lean) + 1 for grade in range(2, count + 1)]
    surplus, holding = total - most - (count - 1), [1] * (count - 1)
    while surplus > 0:
        candidates = [i for i in range(count - 1) if holding[i] < most]
        whole, remaining = sum([loads[i] for i in candidates]), surplus
        for i in candidates:
            addition = min(most - holding[i], max(1, remaining * loads[i] // whole), surplus)
            holding[i] = holding[i] + addition
            surplus = surplus - addition
    return np.array([most] + holding)


def uneven(key, number_of, total, most, slope):
    if number_of == 2:
        one = jax.random.randint(key, (), max(1, total - most), min(most, total - 1) + 1)
        return jnp.stack([one, total - one])
    tallies = jnp.asarray(split_up(number_of, total, most, slope), jnp.int32)
    couples = (number_of - 1) // 2
    donor, sink = tallies[1:1 + 2 * couples:2], tallies[2:2 + 2 * couples:2]
    slack = jnp.minimum(donor - 1, most - sink)
    passed = jax.random.randint(jax.random.fold_in(key, 1), (couples,), 0, 1 << 20) % (slack + 1)
    tallies = tallies.at[1:1 + 2 * couples:2].set(donor - passed).at[2:2 + 2 * couples:2].set(sink + passed)
    return tallies[jax.random.permutation(jax.random.fold_in(key, 2), number_of)]


def centred(own_key, shape, width, limit, shards=(), kind=jnp.bfloat16):
    values = width * jax.random.normal(own_key, shape, jnp.float32)
    if shards:
        values = values * shard_levels(own_key, shape, shards, -0.22, 0.18)
    return jnp.clip(values, -limit, limit).astype(kind)


def setup_inputs(seed: int = 0) -> dict:
    keys = jax.random.split(jax.random.key(seed), 7)
    coarse_basis = centred(keys[0], (NX, NY, FD * C), 1.0, 6.0, ((0, 8), (1, 4)))
    jacobians = centred(keys[1], (JT, ED, ED), ED ** -0.5, 0.21875)
    element_faces = draw_element_faces(jax.random.fold_in(keys[6], 71), 0)
    element_type = set_ends(jax.random.randint(keys[3], (ELEMENTS,), 0, JT), jax.random.fold_in(keys[3], 1), 0, JT - 1).astype(jnp.int32)
    element_count = uneven(keys[4], SUBDOMAINS, SUBDOMAINS * E_CAP * 3 // 4, E_CAP, 1).astype(jnp.int32)
    vertex_ids = draw_vertex_ids(jax.random.fold_in(keys[6], 71), 0)
    return {"coarse_basis": coarse_basis, "jacobians": jacobians, "element_faces": element_faces, "element_type": element_type, "element_count": element_count, "vertex_ids": vertex_ids}


def apply_field(field, element_faces, element_type, element_count, jacobians):
    padded = jnp.pad(field, ((1, 1), (1, 1), (0, 0)))
    totals = jnp.zeros(padded.shape, jnp.float32)
    cells = (FX + 2) * (FY + 2)

    def one_domain(domain, totals):
        domain = jnp.asarray(domain).astype(jnp.int32)
        wide = (domain // N_SLAB).astype(jnp.int32)
        narrow = (domain % N_SLAB).astype(jnp.int32)
        zero = jnp.int32(0)
        start_x = (wide * FX).astype(jnp.int32)
        start_y = (narrow * FY).astype(jnp.int32)
        window = lax.dynamic_slice(padded, (start_x, start_y, zero), (FX + 2, FY + 2, FD * C)).reshape(cells, FD, C)
        first_slot = (domain * E_CAP).astype(jnp.int32)
        faces = lax.dynamic_slice_in_dim(element_faces, first_slot, E_CAP, 0)
        kinds = lax.dynamic_slice_in_dim(element_type, first_slot, E_CAP, 0)
        blocks = window[faces].reshape(E_CAP, 6 * FD, C).astype(jnp.float32)
        matrices = jacobians[kinds].astype(jnp.float32)
        product = jnp.einsum('ekl,elc->ekc', matrices, blocks)
        live = (jnp.arange(E_CAP, dtype=jnp.int32) < element_count[domain]).astype(jnp.float32)
        product = (product * live[:, None, None]).reshape(E_CAP * 6, FD, C)
        local = jnp.zeros((cells, FD, C), jnp.float32).at[faces.reshape(-1)].add(product)
        before = lax.dynamic_slice(totals, (start_x, start_y, zero), (FX + 2, FY + 2, FD * C))
        return lax.dynamic_update_slice(totals, before + local.reshape(FX + 2, FY + 2, FD * C), (start_x, start_y, zero))
    totals = lax.fori_loop(0, N_SUB * N_SLAB, one_domain, totals)
    return totals[1:-1, 1:-1]

def reference(coarse_basis, jacobians, element_faces, element_type, element_count, vertex_ids):
    first_image = apply_field(coarse_basis, element_faces, element_type, element_count, jacobians).astype(jnp.bfloat16)
    second_image = apply_field(first_image, element_faces, element_type, element_count, jacobians).astype(jnp.bfloat16)
    left = coarse_basis.reshape(N_SUB, FX, N_SLAB, FY, FD, C).astype(jnp.float32)
    right = first_image.reshape(N_SUB, FX, N_SLAB, FY, FD, C).astype(jnp.float32)
    local_coarse = jnp.einsum('afbgkc,afbgkd->abcd', left, right) * (1.0 / math.sqrt(FX * FY * FD))
    local_coarse = local_coarse.reshape(N_SUB * N_SLAB, C, C)
    coarse_matrix = jnp.zeros((NV, NV), jnp.float32).at[vertex_ids[:, :, None], vertex_ids[:, None, :]].add(local_coarse)
    return (second_image, coarse_matrix)
```

```python
import functools
import math

import jax
import jax.numpy as jnp
from jax import lax
from jax.experimental import pallas as pl
from jax.experimental.pallas import tpu as pltpu
from jax.sharding import PartitionSpec as P

FX = 4
FY = 8
EX = FX + 2
EY = FY + 2
CELLS = EX * EY
CV = 4
LANES = 128
GROUP = 4
MESH = pl.DeviceIdType.MESH
NT = (((1,), (1,)), ((), ()))


def cell(r, c):
    return r * EY + c


def kernel(
    subs, slabs, slots, dofs,
    x_ref, jac_hbm, meta_ref, ids_ref,
    out_ref, coarse_ref,
    field, jac, pieces, totals, sent, sent_cols, sent_diag, sent_cols_2,
    rim_cols, got_rows, got_cols, got_diag, got_rows_2, got_cols_2,
    dense, got_dense, row_sum, got_sum,
    jac_sem, s0, r0, s1, r1, s2, r2, cs1, cr1, cs2, cr2,
):
    i = lax.axis_index("sub")
    j = lax.axis_index("slab")
    up, down, left, right = i > 0, i < subs - 1, j > 0, j < slabs - 1
    columns = x_ref.shape[1]
    f32 = jnp.float32
    bf16 = jnp.bfloat16

    jac_copy = pltpu.make_async_copy(jac_hbm, jac, jac_sem)
    jac_copy.start()

    barrier = pltpu.get_barrier_semaphore()

    def greet(di, dj):
        pl.semaphore_signal(barrier, inc=1, device_id={"sub": di, "slab": dj}, device_id_type=MESH)

    diagonals = (
        (jnp.logical_and(down, right), i + 1, j + 1),
        (jnp.logical_and(down, left), i + 1, j - 1),
        (jnp.logical_and(up, right), i - 1, j + 1),
        (jnp.logical_and(up, left), i - 1, j - 1),
    )
    from_diagonals = tuple(diagonals[3 - k][0] for k in range(4))

    @pl.loop(1, subs)
    def _(k):
        greet(lax.rem(i + k, subs), j)

    @pl.loop(1, slabs)
    def _(k):
        greet(i, lax.rem(j + k, slabs))

    for there, di, dj in diagonals:
        @pl.when(there)
        def _():
            greet(di, dj)

    @pl.loop(0, pieces.shape[0])
    def _(k):
        pieces[k] = jnp.zeros(pieces.shape[1:], f32)

    blank = jnp.zeros((columns, LANES), bf16)
    for c in (cell(0, 0), cell(0, EY - 1), cell(EX - 1, 0), cell(EX - 1, EY - 1)):
        field[c] = blank

    def fill(there, ref):
        @pl.when(jnp.logical_not(there))
        def _():
            ref[...] = jnp.zeros(ref.shape, ref.dtype)

    sides = (up, down, left, right)
    fill(up, field.at[pl.ds(cell(0, 1), FY)])
    fill(down, field.at[pl.ds(cell(EX - 1, 1), FY)])
    fill(left, rim_cols.at[0])
    fill(right, rim_cols.at[1])
    fill(up, got_rows.at[0])
    fill(down, got_rows.at[1])
    fill(left, got_cols.at[0])
    fill(right, got_cols.at[1])
    fill(up, got_rows_2.at[0])
    fill(down, got_rows_2.at[1])
    fill(left, got_cols_2.at[0])
    fill(right, got_cols_2.at[1])
    for k in range(4):
        fill(from_diagonals[k], got_diag.at[k])

    for r in range(FX):
        for c in range(FY):
            field[cell(r + 1, c + 1)] = x_ref[r * FY + c]

    vertical = up.astype(jnp.int32) + down.astype(jnp.int32)
    sideways = left.astype(jnp.int32) + right.astype(jnp.int32)
    pl.semaphore_wait(barrier, subs - 1 + slabs - 1 + vertical * sideways)

    def remote(src, dst, send, recv, di, dj):
        return pltpu.make_async_remote_copy(
            src_ref=src, dst_ref=dst, send_sem=send, recv_sem=recv,
            device_id={"sub": di, "slab": dj}, device_id_type=MESH,
        )

    def exchange(copies):
        for there, coming, copy in copies:
            @pl.when(there)
            def _():
                copy.start()

    def arrive(copies):
        for there, coming, copy in copies:
            @pl.when(coming)
            def _():
                copy.wait_recv()

    def leave(copies):
        for there, coming, copy in copies:
            @pl.when(there)
            def _():
                copy.wait_send()

    x_cols = x_ref.reshape(FX, FY, columns, LANES)
    first = (
        (up, down, remote(x_ref.at[pl.ds(0, FY)], field.at[pl.ds(cell(EX - 1, 1), FY)],
                          s0.at[0], r0.at[0], i - 1, j)),
        (down, up, remote(x_ref.at[pl.ds((FX - 1) * FY, FY)], field.at[pl.ds(cell(0, 1), FY)],
                          s0.at[1], r0.at[1], i + 1, j)),
        (left, right, remote(x_cols.at[:, 0], rim_cols.at[1], s0.at[2], r0.at[2], i, j - 1)),
        (right, left, remote(x_cols.at[:, FY - 1], rim_cols.at[0], s0.at[3], r0.at[3], i, j + 1)),
    )
    exchange(first)
    jac_copy.wait()
    arrive(first)
    for r in range(FX):
        field[cell(r + 1, 0)] = rim_cols[0, r]
        field[cell(r + 1, EY - 1)] = rim_cols[1, r]

    def apply():
        @pl.loop(0, slots // GROUP)
        def _(g):
            for k in range(GROUP):
                e = g * GROUP + k
                x = jnp.concatenate(
                    [field[meta_ref[e * 6 + p]][:, :dofs] for p in range(6)], axis=1
                )
                y = lax.dot_general(
                    x, jac[meta_ref[slots * 6 + e]], NT, preferred_element_type=f32
                )
                for p in range(6):
                    pieces[1 + e * 6 + p, :, :dofs] = y[:, p * dofs : (p + 1) * dofs]

        @pl.loop(0, CELLS)
        def _(c):
            base = slots * 7 + c * slots
            total = pieces[meta_ref[base]]
            for e in range(1, slots):
                total = total + pieces[meta_ref[base + e]]
            totals[c] = total
            sent[c] = total.astype(bf16)

    apply()
    for r in range(FX):
        for k in range(2):
            sent_cols[0, r, k] = sent[cell(r + 1, k)]
            sent_cols[1, r, k] = sent[cell(r + 1, FY + k)]
    corners = (
        (cell(FX, EY - 1), cell(EX - 1, FY)),
        (cell(FX, 0), cell(EX - 1, 1)),
        (cell(1, EY - 1), cell(0, FY)),
        (cell(1, 0), cell(0, 1)),
    )
    for k in range(4):
        for n in range(2):
            sent_diag[k, n] = sent[corners[k][n]]
    span = EY + FY
    second = (
        (up, down, remote(sent.at[pl.ds(cell(0, 1), span)], got_rows.at[1],
                          s1.at[0], r1.at[0], i - 1, j)),
        (down, up, remote(sent.at[pl.ds(cell(FX, 1), span)], got_rows.at[0],
                          s1.at[1], r1.at[1], i + 1, j)),
        (left, right, remote(sent_cols.at[0], got_cols.at[1], s1.at[2], r1.at[2], i, j - 1)),
        (right, left, remote(sent_cols.at[1], got_cols.at[0], s1.at[3], r1.at[3], i, j + 1)),
    ) + tuple(
        (diagonals[k][0], from_diagonals[k],
         remote(sent_diag.at[k], got_diag.at[k], s1.at[4 + k], r1.at[4 + k],
                diagonals[k][1], diagonals[k][2]))
        for k in range(4)
    )
    exchange(second)
    leave(first)
    arrive(second)

    def wide(ref, *at):
        return ref[at].astype(f32)

    for r in range(1, FX + 1):
        for c in range(1, FY + 1):
            v = totals[cell(r, c)]
            if r == 1:
                v = v + wide(got_rows, 0, EY + c - 1)
            if r == FX:
                v = v + wide(got_rows, 1, c - 1)
            if c == 1:
                v = v + wide(got_cols, 0, r - 1, 1)
            if c == FY:
                v = v + wide(got_cols, 1, r - 1, 0)
            field[cell(r, c)] = v.astype(bf16)

    def keep(there, c, v):
        field[c] = jnp.where(there, v, 0.0).astype(bf16)

    for c in range(1, FY + 1):
        v = totals[cell(0, c)] + wide(got_rows, 0, c - 1)
        w = totals[cell(EX - 1, c)] + wide(got_rows, 1, EY + c - 1)
        if c == 1:
            v, w = v + wide(got_diag, 0, 0), w + wide(got_diag, 2, 0)
        if c == FY:
            v, w = v + wide(got_diag, 1, 0), w + wide(got_diag, 3, 0)
        keep(up, cell(0, c), v)
        keep(down, cell(EX - 1, c), w)
    for r in range(1, FX + 1):
        v = totals[cell(r, 0)] + wide(got_cols, 0, r - 1, 0)
        w = totals[cell(r, EY - 1)] + wide(got_cols, 1, r - 1, 1)
        if r == 1:
            v, w = v + wide(got_diag, 0, 1), w + wide(got_diag, 1, 1)
        if r == FX:
            v, w = v + wide(got_diag, 2, 1), w + wide(got_diag, 3, 1)
        keep(left, cell(r, 0), v)
        keep(right, cell(r, EY - 1), w)

    local = jnp.zeros((columns, columns), f32)
    for r in range(FX):
        for c in range(FY):
            local = local + lax.dot_general(
                x_ref[r * FY + c], field[cell(r + 1, c + 1)], NT, preferred_element_type=f32
            )
    local = local * (1.0 / math.sqrt(FX * FY * dofs))
    ids = ids_ref[...]
    width = dense.shape[1]
    spots = lax.broadcasted_iota(jnp.int32, (width, columns), 0)
    one_hot = jnp.where(spots == ids, 1.0, 0.0).astype(f32)
    rows = lax.broadcasted_iota(jnp.int32, (8 * subs, columns), 0)
    spot = jnp.where(rows % 8 < CV, rows // 8 * CV + rows % 8, -1)
    row_hot = jnp.where(spot == ids, 1.0, 0.0).astype(f32)
    placed = lax.dot_general(
        local, one_hot, NT, precision=lax.Precision.HIGHEST, preferred_element_type=f32
    )
    dense[...] = jnp.dot(
        row_hot, placed, precision=lax.Precision.HIGHEST, preferred_element_type=f32
    )

    def block(s):
        return dense.at[pl.ds(pl.multiple_of(s * 8, 8), 8)]

    def to_sub(s):
        return remote(block(s), got_dense.at[i], cs1.at[s], cr1.at[i], s, j)

    def from_sub(s):
        return remote(block(s), got_dense.at[s], cs1.at[s], cr1.at[s], s, j)

    def to_slab(s):
        return remote(row_sum, got_sum.at[j], cs2.at[s], cr2.at[j], i, s)

    def from_slab(s):
        return remote(row_sum, got_sum.at[s], cs2.at[s], cr2.at[s], i, s)

    @pl.loop(1, subs)
    def _(k):
        to_sub(lax.rem(i + k, subs)).start()

    leave(second)
    apply()

    for r in range(FX):
        sent_cols_2[0, r] = sent[cell(r + 1, 0)]
        sent_cols_2[1, r] = sent[cell(r + 1, EY - 1)]
    third = (
        (up, down, remote(sent.at[pl.ds(cell(0, 1), FY)], got_rows_2.at[1],
                          s2.at[0], r2.at[0], i - 1, j)),
        (down, up, remote(sent.at[pl.ds(cell(EX - 1, 1), FY)], got_rows_2.at[0],
                          s2.at[1], r2.at[1], i + 1, j)),
        (left, right, remote(sent_cols_2.at[0], got_cols_2.at[1], s2.at[2], r2.at[2], i, j - 1)),
        (right, left, remote(sent_cols_2.at[1], got_cols_2.at[0], s2.at[3], r2.at[3], i, j + 1)),
    )
    exchange(third)

    row_sum[...] = block(i)[...]

    @pl.loop(1, subs)
    def _(k):
        s = lax.rem(i + k, subs)
        from_sub(s).wait_recv()
        row_sum[...] += got_dense[s]

    @pl.loop(1, slabs)
    def _(k):
        to_slab(lax.rem(j + k, slabs)).start()

    arrive(third)
    for r in range(1, FX + 1):
        for c in range(1, FY + 1):
            v = totals[cell(r, c)]
            if r == 1:
                v = v + wide(got_rows_2, 0, c - 1)
            if r == FX:
                v = v + wide(got_rows_2, 1, c - 1)
            if c == 1:
                v = v + wide(got_cols_2, 0, r - 1)
            if c == FY:
                v = v + wide(got_cols_2, 1, r - 1)
            out_ref[(r - 1) * FY + c - 1] = v.astype(bf16)

    coarse_ref[...] = row_sum[...]

    @pl.loop(1, slabs)
    def _(k):
        s = lax.rem(j + k, slabs)
        from_slab(s).wait_recv()
        coarse_ref[...] += got_sum[s]

    leave(third)

    @pl.loop(1, subs)
    def _(k):
        to_sub(lax.rem(i + k, subs)).wait_send()

    @pl.loop(1, slabs)
    def _(k):
        to_slab(lax.rem(j + k, slabs)).wait_send()


def body(coarse_basis, jacobians, element_faces, element_type, element_count, vertex_ids):
    subs, slabs = lax.axis_size("sub"), lax.axis_size("slab")
    dofs = jacobians.shape[1] // 6
    columns = coarse_basis.shape[2] // dofs
    slots = element_faces.shape[0]
    vertex_total = CV * subs
    width = -(-vertex_total // LANES) * LANES
    f32, bf16 = jnp.float32, jnp.bfloat16

    x = coarse_basis.reshape(FX * FY, dofs, columns).transpose(0, 2, 1)
    x = jnp.pad(x, ((0, 0), (0, 0), (0, LANES - dofs)))
    slot = jnp.arange(slots, dtype=jnp.int32)
    which = slot[:, None] * 6 + jnp.arange(1, 7, dtype=jnp.int32)[None, :]
    which = jnp.where((slot < element_count[0])[:, None], which, 0)
    cells = jnp.arange(CELLS, dtype=jnp.int32)
    inverse = jnp.sum(
        jnp.where(element_faces[None] == cells[:, None, None], which[None], 0), axis=2
    )
    meta = jnp.concatenate([element_faces.reshape(-1), element_type, inverse.reshape(-1)])

    def block(*lead):
        return pltpu.VMEM((*lead, columns, LANES), bf16)

    vmem = pl.BlockSpec(memory_space=pltpu.VMEM)
    dma = pltpu.SemaphoreType.DMA
    out, coarse = pl.pallas_call(
        functools.partial(kernel, subs, slabs, slots, dofs),
        out_shape=(
            jax.ShapeDtypeStruct((FX * FY, columns, LANES), bf16),
            jax.ShapeDtypeStruct((8, width), f32),
        ),
        in_specs=[
            vmem,
            pl.BlockSpec(memory_space=pl.ANY),
            pl.BlockSpec(memory_space=pltpu.SMEM),
            vmem,
        ],
        out_specs=(vmem, vmem),
        scratch_shapes=[
            block(CELLS),
            pltpu.VMEM(jacobians.shape, bf16),
            pltpu.VMEM((1 + 6 * slots, columns, LANES), f32),
            pltpu.VMEM((CELLS, columns, LANES), f32),
            block(CELLS),
            block(2, FX, 2),
            block(4, 2),
            block(2, FX),
            block(2, FX),
            block(2, EY + FY),
            block(2, FX, 2),
            block(4, 2),
            block(2, FY),
            block(2, FX),
            pltpu.VMEM((8 * subs, width), f32),
            pltpu.VMEM((subs, 8, width), f32),
            pltpu.VMEM((8, width), f32),
            pltpu.VMEM((slabs, 8, width), f32),
            dma,
            dma((4,)), dma((4,)),
            dma((8,)), dma((8,)),
            dma((4,)), dma((4,)),
            dma((subs,)), dma((subs,)),
            dma((slabs,)), dma((slabs,)),
        ],
        compiler_params=pltpu.CompilerParams(
            collective_id=0, has_side_effects=True, vmem_limit_bytes=40 * 1024 * 1024
        ),
        cost_estimate=pl.CostEstimate(
            flops=4 * slots * (6 * dofs) ** 2 * columns,
            bytes_accessed=2 * jacobians.size,
            transcendentals=0,
        ),
    )(x, jacobians, meta, vertex_ids)
    out = out[:, :, :dofs].transpose(0, 2, 1).reshape(FX, FY, dofs * columns)
    return out, coarse[:CV, :vertex_total]


def solution(mesh):
    return jax.shard_map(
        body,
        mesh=mesh,
        in_specs=(
            P("sub", "slab", None),
            P(),
            P(("sub", "slab"), None),
            P(("sub", "slab")),
            P(("sub", "slab")),
            P(("sub", "slab"), None),
        ),
        out_specs=(P("sub", "slab", None), P("sub", None)),
        check_vma=False,
    )
```

```python
import functools
import math

import jax
import jax.numpy as jnp
from jax import lax
from jax.experimental import pallas as pl
from jax.experimental.pallas import tpu as pltpu
from jax.sharding import PartitionSpec as P

FX = 4
FY = 8
EX = FX + 2
EY = FY + 2
CELLS = EX * EY
CV = 4
TYPES = 4
LANES = 128
GROUP = 4
GATHER = 4
MESH = pl.DeviceIdType.MESH
NT = (((1,), (1,)), ((), ()))


def cell(r, c):
    return r * EY + c


def group_count(slots):
    return (slots + TYPES * (GROUP - 1)) // GROUP


def index_lists(faces, kinds, count):
    slots, groups = faces.shape[0], group_count(faces.shape[0])
    i32 = jnp.int32
    slot = jnp.arange(slots, dtype=i32)
    live = slot < count
    kind = jnp.where(live, kinds, TYPES)
    earlier = slot[None, :] < slot[:, None]
    same = kind[None, :] == kind[:, None]
    place_in_kind = jnp.sum(jnp.where(same & earlier, 1, 0), axis=1)
    place = place_in_kind + jnp.sum(jnp.where(kind[None, :] < kind[:, None], 1, 0), axis=1)
    types = jnp.arange(TYPES, dtype=i32)
    number = jnp.sum(jnp.where(kind[None, :] == types[:, None], 1, 0), axis=1)
    needed = (number + GROUP - 1) // GROUP
    before = types[None, :] < types[:, None]
    first_group = jnp.sum(jnp.where(before, needed[None, :], 0), axis=1)
    first_place = jnp.sum(jnp.where(before, number[None, :], 0), axis=1)
    group = jnp.arange(groups, dtype=i32)
    inside = (group[:, None] >= first_group[None, :]) & (
        group[:, None] < (first_group + needed)[None, :]
    )
    group_type = jnp.sum(jnp.where(inside, types[None, :], 0), axis=1)
    group_start = jnp.sum(
        jnp.where(inside, first_place[None, :] + GROUP * (group[:, None] - first_group[None, :]), 0),
        axis=1,
    )
    offset = jnp.sum(
        jnp.where(kind[:, None] == types[None, :], GROUP * first_group[None, :], 0), axis=1
    )
    number_of_piece = (offset + place_in_kind)[:, None] * 6 + jnp.arange(1, 7, dtype=i32)[None, :]
    number_of_piece = jnp.where(live[:, None], number_of_piece, 0)
    cells = jnp.arange(CELLS, dtype=i32)
    inverse = jnp.sum(
        jnp.where(faces[None] == cells[:, None, None], number_of_piece[None], 0), axis=2
    )
    ordered = jnp.sum(
        jnp.where((place[None, :] == slot[:, None])[:, :, None], faces[None], 0), axis=1
    )
    return jnp.concatenate([ordered.reshape(-1), group_type, group_start, inverse.reshape(-1)])


def kernel(
    subs, slabs, slots, dofs,
    x_ref, jac_hbm, meta_ref, ids_ref,
    out_ref, coarse_ref,
    field, jac, stacked, pieces, totals, sent, sent_cols, sent_diag, sent_cols_2,
    rim_cols, got_rows, got_cols, got_diag, got_rows_2, got_cols_2,
    dense, got_dense, row_sum, got_sum,
    jac_sem, s0, r0, s1, r1, s2, r2, cs1, cr1, cs2, cr2,
):
    i = lax.axis_index("sub")
    j = lax.axis_index("slab")
    up, down, left, right = i > 0, i < subs - 1, j > 0, j < slabs - 1
    columns = x_ref.shape[1]
    f32 = jnp.float32
    bf16 = jnp.bfloat16

    jac_copy = pltpu.make_async_copy(jac_hbm, jac, jac_sem)
    jac_copy.start()

    barrier = pltpu.get_barrier_semaphore()

    def greet(di, dj):
        pl.semaphore_signal(barrier, inc=1, device_id={"sub": di, "slab": dj}, device_id_type=MESH)

    diagonals = (
        (jnp.logical_and(down, right), i + 1, j + 1),
        (jnp.logical_and(down, left), i + 1, j - 1),
        (jnp.logical_and(up, right), i - 1, j + 1),
        (jnp.logical_and(up, left), i - 1, j - 1),
    )
    from_diagonals = tuple(diagonals[3 - k][0] for k in range(4))

    @pl.loop(1, subs)
    def _(k):
        greet(lax.rem(i + k, subs), j)

    @pl.loop(1, slabs)
    def _(k):
        greet(i, lax.rem(j + k, slabs))

    for there, di, dj in diagonals:
        @pl.when(there)
        def _():
            greet(di, dj)

    @pl.loop(0, pieces.shape[0])
    def _(k):
        pieces[k] = jnp.zeros(pieces.shape[1:], f32)

    for k in range(GROUP):
        stacked[slots + k] = jnp.zeros(stacked.shape[1:], bf16)
    blank = jnp.zeros((columns, LANES), bf16)
    for c in (cell(0, 0), cell(0, EY - 1), cell(EX - 1, 0), cell(EX - 1, EY - 1)):
        field[c] = blank

    def fill(there, ref):
        @pl.when(jnp.logical_not(there))
        def _():
            ref[...] = jnp.zeros(ref.shape, ref.dtype)

    sides = (up, down, left, right)
    fill(up, field.at[pl.ds(cell(0, 1), FY)])
    fill(down, field.at[pl.ds(cell(EX - 1, 1), FY)])
    fill(left, rim_cols.at[0])
    fill(right, rim_cols.at[1])
    fill(up, got_rows.at[0])
    fill(down, got_rows.at[1])
    fill(left, got_cols.at[0])
    fill(right, got_cols.at[1])
    fill(up, got_rows_2.at[0])
    fill(down, got_rows_2.at[1])
    fill(left, got_cols_2.at[0])
    fill(right, got_cols_2.at[1])
    for k in range(4):
        fill(from_diagonals[k], got_diag.at[k])

    for r in range(FX):
        for c in range(FY):
            field[cell(r + 1, c + 1)] = x_ref[r * FY + c]

    vertical = up.astype(jnp.int32) + down.astype(jnp.int32)
    sideways = left.astype(jnp.int32) + right.astype(jnp.int32)
    pl.semaphore_wait(barrier, subs - 1 + slabs - 1 + vertical * sideways)

    def remote(src, dst, send, recv, di, dj):
        return pltpu.make_async_remote_copy(
            src_ref=src, dst_ref=dst, send_sem=send, recv_sem=recv,
            device_id={"sub": di, "slab": dj}, device_id_type=MESH,
        )

    def exchange(copies):
        for there, coming, copy in copies:
            @pl.when(there)
            def _():
                copy.start()

    def arrive(copies):
        for there, coming, copy in copies:
            @pl.when(coming)
            def _():
                copy.wait_recv()

    def leave(copies):
        for there, coming, copy in copies:
            @pl.when(there)
            def _():
                copy.wait_send()

    x_cols = x_ref.reshape(FX, FY, columns, LANES)
    first = (
        (up, down, remote(x_ref.at[pl.ds(0, FY)], field.at[pl.ds(cell(EX - 1, 1), FY)],
                          s0.at[0], r0.at[0], i - 1, j)),
        (down, up, remote(x_ref.at[pl.ds((FX - 1) * FY, FY)], field.at[pl.ds(cell(0, 1), FY)],
                          s0.at[1], r0.at[1], i + 1, j)),
        (left, right, remote(x_cols.at[:, 0], rim_cols.at[1], s0.at[2], r0.at[2], i, j - 1)),
        (right, left, remote(x_cols.at[:, FY - 1], rim_cols.at[0], s0.at[3], r0.at[3], i, j + 1)),
    )
    exchange(first)
    jac_copy.wait()
    arrive(first)
    for r in range(FX):
        field[cell(r + 1, 0)] = rim_cols[0, r]
        field[cell(r + 1, EY - 1)] = rim_cols[1, r]

    rows_in = columns * GROUP
    groups = group_count(slots)
    at_type = slots * 6
    at_start = at_type + groups
    at_inverse = at_start + groups

    def apply():
        @pl.loop(0, slots // GATHER)
        def _(g):
            for k in range(GATHER):
                e = g * GATHER + k
                x = jnp.concatenate(
                    [field[meta_ref[e * 6 + p]][:, :dofs] for p in range(6)], axis=1
                )
                stacked[e] = x

        @pl.loop(0, groups)
        def _(g):
            start = meta_ref[at_start + g]
            x = stacked[pl.ds(start, GROUP)].reshape(rows_in, 6 * dofs)
            y = lax.dot_general(
                x, jac[meta_ref[at_type + g]], NT, preferred_element_type=f32
            )
            for k in range(GROUP):
                for p in range(6):
                    pieces[1 + (g * GROUP + k) * 6 + p, :, :dofs] = y[
                        k * columns : (k + 1) * columns, p * dofs : (p + 1) * dofs
                    ]

        @pl.loop(0, CELLS)
        def _(c):
            base = at_inverse + c * slots
            total = pieces[meta_ref[base]]
            for e in range(1, slots):
                total = total + pieces[meta_ref[base + e]]
            totals[c] = total
            sent[c] = total.astype(bf16)

    apply()
    for r in range(FX):
        for k in range(2):
            sent_cols[0, r, k] = sent[cell(r + 1, k)]
            sent_cols[1, r, k] = sent[cell(r + 1, FY + k)]
    corners = (
        (cell(FX, EY - 1), cell(EX - 1, FY)),
        (cell(FX, 0), cell(EX - 1, 1)),
        (cell(1, EY - 1), cell(0, FY)),
        (cell(1, 0), cell(0, 1)),
    )
    for k in range(4):
        for n in range(2):
            sent_diag[k, n] = sent[corners[k][n]]
    span = EY + FY
    second = (
        (up, down, remote(sent.at[pl.ds(cell(0, 1), span)], got_rows.at[1],
                          s1.at[0], r1.at[0], i - 1, j)),
        (down, up, remote(sent.at[pl.ds(cell(FX, 1), span)], got_rows.at[0],
                          s1.at[1], r1.at[1], i + 1, j)),
        (left, right, remote(sent_cols.at[0], got_cols.at[1], s1.at[2], r1.at[2], i, j - 1)),
        (right, left, remote(sent_cols.at[1], got_cols.at[0], s1.at[3], r1.at[3], i, j + 1)),
    ) + tuple(
        (diagonals[k][0], from_diagonals[k],
         remote(sent_diag.at[k], got_diag.at[k], s1.at[4 + k], r1.at[4 + k],
                diagonals[k][1], diagonals[k][2]))
        for k in range(4)
    )
    exchange(second)
    leave(first)
    arrive(second)

    def wide(ref, *at):
        return ref[at].astype(f32)

    for r in range(1, FX + 1):
        for c in range(1, FY + 1):
            v = totals[cell(r, c)]
            if r == 1:
                v = v + wide(got_rows, 0, EY + c - 1)
            if r == FX:
                v = v + wide(got_rows, 1, c - 1)
            if c == 1:
                v = v + wide(got_cols, 0, r - 1, 1)
            if c == FY:
                v = v + wide(got_cols, 1, r - 1, 0)
            field[cell(r, c)] = v.astype(bf16)

    def keep(there, c, v):
        field[c] = jnp.where(there, v, 0.0).astype(bf16)

    for c in range(1, FY + 1):
        v = totals[cell(0, c)] + wide(got_rows, 0, c - 1)
        w = totals[cell(EX - 1, c)] + wide(got_rows, 1, EY + c - 1)
        if c == 1:
            v, w = v + wide(got_diag, 0, 0), w + wide(got_diag, 2, 0)
        if c == FY:
            v, w = v + wide(got_diag, 1, 0), w + wide(got_diag, 3, 0)
        keep(up, cell(0, c), v)
        keep(down, cell(EX - 1, c), w)
    for r in range(1, FX + 1):
        v = totals[cell(r, 0)] + wide(got_cols, 0, r - 1, 0)
        w = totals[cell(r, EY - 1)] + wide(got_cols, 1, r - 1, 1)
        if r == 1:
            v, w = v + wide(got_diag, 0, 1), w + wide(got_diag, 1, 1)
        if r == FX:
            v, w = v + wide(got_diag, 2, 1), w + wide(got_diag, 3, 1)
        keep(left, cell(r, 0), v)
        keep(right, cell(r, EY - 1), w)

    own = range(FX * FY)
    local = lax.dot_general(
        jnp.concatenate([x_ref[k] for k in own], axis=1),
        jnp.concatenate([field[cell(k // FY + 1, k % FY + 1)] for k in own], axis=1),
        NT, preferred_element_type=f32,
    )
    local = local * (1.0 / math.sqrt(FX * FY * dofs))
    ids = ids_ref[...]
    width = dense.shape[1]
    spots = lax.broadcasted_iota(jnp.int32, (width, columns), 0)
    one_hot = jnp.where(spots == ids, 1.0, 0.0).astype(f32)
    rows = lax.broadcasted_iota(jnp.int32, (8 * subs, columns), 0)
    spot = jnp.where(rows % 8 < CV, rows // 8 * CV + rows % 8, -1)
    row_hot = jnp.where(spot == ids, 1.0, 0.0).astype(f32)
    placed = lax.dot_general(
        local, one_hot, NT, precision=lax.Precision.HIGHEST, preferred_element_type=f32
    )
    dense[...] = jnp.dot(
        row_hot, placed, precision=lax.Precision.HIGHEST, preferred_element_type=f32
    )

    def block(s):
        return dense.at[pl.ds(pl.multiple_of(s * 8, 8), 8)]

    def to_sub(s):
        return remote(block(s), got_dense.at[i], cs1.at[s], cr1.at[i], s, j)

    def from_sub(s):
        return remote(block(s), got_dense.at[s], cs1.at[s], cr1.at[s], s, j)

    def to_slab(s):
        return remote(row_sum, got_sum.at[j], cs2.at[s], cr2.at[j], i, s)

    def from_slab(s):
        return remote(row_sum, got_sum.at[s], cs2.at[s], cr2.at[s], i, s)

    @pl.loop(1, subs)
    def _(k):
        to_sub(lax.rem(i + k, subs)).start()

    leave(second)
    apply()

    for r in range(FX):
        sent_cols_2[0, r] = sent[cell(r + 1, 0)]
        sent_cols_2[1, r] = sent[cell(r + 1, EY - 1)]
    third = (
        (up, down, remote(sent.at[pl.ds(cell(0, 1), FY)], got_rows_2.at[1],
                          s2.at[0], r2.at[0], i - 1, j)),
        (down, up, remote(sent.at[pl.ds(cell(EX - 1, 1), FY)], got_rows_2.at[0],
                          s2.at[1], r2.at[1], i + 1, j)),
        (left, right, remote(sent_cols_2.at[0], got_cols_2.at[1], s2.at[2], r2.at[2], i, j - 1)),
        (right, left, remote(sent_cols_2.at[1], got_cols_2.at[0], s2.at[3], r2.at[3], i, j + 1)),
    )
    exchange(third)

    row_sum[...] = block(i)[...]

    @pl.loop(1, subs)
    def _(k):
        s = lax.rem(i + k, subs)
        from_sub(s).wait_recv()
        row_sum[...] += got_dense[s]

    @pl.loop(1, slabs)
    def _(k):
        to_slab(lax.rem(j + k, slabs)).start()

    arrive(third)
    for r in range(1, FX + 1):
        for c in range(1, FY + 1):
            v = totals[cell(r, c)]
            if r == 1:
                v = v + wide(got_rows_2, 0, c - 1)
            if r == FX:
                v = v + wide(got_rows_2, 1, c - 1)
            if c == 1:
                v = v + wide(got_cols_2, 0, r - 1)
            if c == FY:
                v = v + wide(got_cols_2, 1, r - 1)
            out_ref[(r - 1) * FY + c - 1] = v.astype(bf16)

    coarse_ref[...] = row_sum[...]

    @pl.loop(1, slabs)
    def _(k):
        s = lax.rem(j + k, slabs)
        from_slab(s).wait_recv()
        coarse_ref[...] += got_sum[s]

    leave(third)

    @pl.loop(1, subs)
    def _(k):
        to_sub(lax.rem(i + k, subs)).wait_send()

    @pl.loop(1, slabs)
    def _(k):
        to_slab(lax.rem(j + k, slabs)).wait_send()


def body(coarse_basis, jacobians, element_faces, element_type, element_count, vertex_ids):
    subs, slabs = lax.axis_size("sub"), lax.axis_size("slab")
    dofs = jacobians.shape[1] // 6
    columns = coarse_basis.shape[2] // dofs
    slots = element_faces.shape[0]
    vertex_total = CV * subs
    width = -(-vertex_total // LANES) * LANES
    f32, bf16 = jnp.float32, jnp.bfloat16

    x = coarse_basis.reshape(FX * FY, dofs, columns).transpose(0, 2, 1)
    x = jnp.pad(x, ((0, 0), (0, 0), (0, LANES - dofs)))
    groups = group_count(slots)
    meta = index_lists(element_faces, element_type, element_count[0])

    def block(*lead):
        return pltpu.VMEM((*lead, columns, LANES), bf16)

    vmem = pl.BlockSpec(memory_space=pltpu.VMEM)
    dma = pltpu.SemaphoreType.DMA
    out, coarse = pl.pallas_call(
        functools.partial(kernel, subs, slabs, slots, dofs),
        out_shape=(
            jax.ShapeDtypeStruct((FX * FY, columns, LANES), bf16),
            jax.ShapeDtypeStruct((8, width), f32),
        ),
        in_specs=[
            vmem,
            pl.BlockSpec(memory_space=pl.ANY),
            pl.BlockSpec(memory_space=pltpu.SMEM),
            vmem,
        ],
        out_specs=(vmem, vmem),
        scratch_shapes=[
            block(CELLS),
            pltpu.VMEM(jacobians.shape, bf16),
            pltpu.VMEM((slots + GROUP, columns, 6 * dofs), bf16),
            pltpu.VMEM((1 + 6 * GROUP * groups, columns, LANES), f32),
            pltpu.VMEM((CELLS, columns, LANES), f32),
            block(CELLS),
            block(2, FX, 2),
            block(4, 2),
            block(2, FX),
            block(2, FX),
            block(2, EY + FY),
            block(2, FX, 2),
            block(4, 2),
            block(2, FY),
            block(2, FX),
            pltpu.VMEM((8 * subs, width), f32),
            pltpu.VMEM((subs, 8, width), f32),
            pltpu.VMEM((8, width), f32),
            pltpu.VMEM((slabs, 8, width), f32),
            dma,
            dma((4,)), dma((4,)),
            dma((8,)), dma((8,)),
            dma((4,)), dma((4,)),
            dma((subs,)), dma((subs,)),
            dma((slabs,)), dma((slabs,)),
        ],
        compiler_params=pltpu.CompilerParams(
            collective_id=0, has_side_effects=True, vmem_limit_bytes=40 * 1024 * 1024
        ),
        cost_estimate=pl.CostEstimate(
            flops=4 * slots * (6 * dofs) ** 2 * columns,
            bytes_accessed=2 * jacobians.size,
            transcendentals=0,
        ),
    )(x, jacobians, meta, vertex_ids)
    out = out[:, :, :dofs].transpose(0, 2, 1).reshape(FX, FY, dofs * columns)
    return out, coarse[:CV, :vertex_total]


def solution(mesh):
    return jax.shard_map(
        body,
        mesh=mesh,
        in_specs=(
            P("sub", "slab", None),
            P(),
            P(("sub", "slab"), None),
            P(("sub", "slab")),
            P(("sub", "slab")),
            P(("sub", "slab"), None),
        ),
        out_specs=(P("sub", "slab", None), P("sub", None)),
        check_vma=False,
    )
```

```python
import functools
import math

import jax
import jax.numpy as jnp
from jax import lax
from jax.experimental import pallas as pl
from jax.experimental.pallas import tpu as pltpu
from jax.sharding import PartitionSpec as P

FX = 4
FY = 8
EX = FX + 2
EY = FY + 2
CELLS = EX * EY
CV = 4
TYPES = 4
LANES = 128
GROUP = 4
GATHER = 4
SUMS = 8
SPREAD = 4
MESH = pl.DeviceIdType.MESH
NT = (((1,), (1,)), ((), ()))


def cell(r, c):
    return r * EY + c


def group_count(slots):
    return (slots + TYPES * (GROUP - 1)) // GROUP


def index_lists(faces_ref, kinds_ref, count, lists):
    slots, groups = faces_ref.shape[1], group_count(faces_ref.shape[1])
    i32 = jnp.int32

    def iota(rows, cols, axis):
        return lax.broadcasted_iota(i32, (rows, cols), axis)

    def count_of(mask, axis):
        return jnp.sum(jnp.where(mask, 1, 0), axis=axis, keepdims=True)

    def as_column(row):
        n = row.shape[1]
        return jnp.sum(jnp.where(iota(n, n, 0) == iota(n, n, 1), row, 0), axis=1, keepdims=True)

    def put(lane, column):
        lists[pl.ds(0, column.shape[0]), lane : lane + 1] = column

    lists[...] = jnp.zeros(lists.shape, i32)
    live = iota(1, slots, 1) < count
    kind = jnp.where(live, kinds_ref[...], TYPES)
    kind_col = as_column(kind)
    earlier = iota(slots, slots, 0) < iota(slots, slots, 1)
    in_kind = count_of((kind_col == kind) & earlier, 0)
    place = in_kind + count_of(kind_col < kind, 0)
    group = iota(groups, 1, 0)
    group_type = jnp.zeros((groups, 1), i32)
    group_start = jnp.zeros((groups, 1), i32)
    position = in_kind
    first_group = jnp.zeros((1, 1), i32)
    first_place = jnp.zeros((1, 1), i32)
    for t in range(TYPES):
        number = count_of(kind == t, 1)
        needed = lax.shift_right_logical(number + (GROUP - 1), 2)
        inside = (group >= first_group) & (group < first_group + needed)
        group_type = jnp.where(inside, t, group_type)
        group_start = jnp.where(inside, first_place + GROUP * (group - first_group), group_start)
        position = position + jnp.where(kind == t, GROUP * first_group, 0)
        first_group = first_group + needed
        first_place = first_place + number
    faces = [faces_ref[p : p + 1, :] for p in range(6)]
    cells = jnp.concatenate([jnp.where(live, f, CELLS) for f in faces], axis=1)
    piece = jnp.concatenate([position * 6 + p for p in range(6)], axis=1)
    total = 6 * slots
    cells_col = as_column(cells)
    before = iota(total, total, 0) < iota(total, total, 1)
    in_cell = count_of((cells_col == cells) & before, 0)
    rank = in_cell + count_of(cells_col < cells, 0)
    chosen = rank == iota(total, 1, 0)
    put(0, jnp.sum(jnp.where(chosen, piece, 0), axis=1, keepdims=True))
    put(1, jnp.sum(jnp.where(chosen, jnp.where(in_cell == 0, 1, 0), 0), axis=1, keepdims=True))
    spot = iota(CELLS, 1, 0)
    upto = count_of(cells <= spot, 1)
    put(2, jnp.where(count_of(cells == spot, 1) > 0, upto, 0))
    taken = place == iota(slots, 1, 0)
    for p in range(6):
        put(3 + p, jnp.sum(jnp.where(taken, faces[p], 0), axis=1, keepdims=True))
    put(9, group_type)
    put(10, group_start)


def kernel(
    subs, slabs, slots, dofs,
    x_ref, jac, faces_ref, kinds_ref, count_ref, ids_ref,
    out_ref, coarse_ref,
    field, lists, meta_ref, stacked, pieces, running, totals, sent, sent_cols, sent_diag, sent_cols_2,
    rim_cols, got_rows, got_cols, got_diag, got_rows_2, got_cols_2,
    dense, got_dense, row_sum, got_sum,
    list_sem, s0, r0, s1, r1, s2, r2, cs1, cr1, cs2, cr2,
):
    i = lax.axis_index("sub")
    j = lax.axis_index("slab")
    up, down, left, right = i > 0, i < subs - 1, j > 0, j < slabs - 1
    columns = x_ref.shape[1]
    f32 = jnp.float32
    bf16 = jnp.bfloat16

    barrier = pltpu.get_barrier_semaphore()

    def greet(di, dj):
        pl.semaphore_signal(barrier, inc=1, device_id={"sub": di, "slab": dj}, device_id_type=MESH)

    diagonals = (
        (jnp.logical_and(down, right), i + 1, j + 1),
        (jnp.logical_and(down, left), i + 1, j - 1),
        (jnp.logical_and(up, right), i - 1, j + 1),
        (jnp.logical_and(up, left), i - 1, j - 1),
    )
    from_diagonals = tuple(diagonals[3 - k][0] for k in range(4))

    @pl.loop(1, subs)
    def _(k):
        greet(lax.rem(i + k, subs), j)

    @pl.loop(1, slabs)
    def _(k):
        greet(i, lax.rem(j + k, slabs))

    for there, di, dj in diagonals:
        @pl.when(there)
        def _():
            greet(di, dj)

    index_lists(faces_ref, kinds_ref, count_ref[0], lists)
    list_copy = pltpu.make_async_copy(lists, meta_ref, list_sem)
    list_copy.start()

    @pl.loop(0, pieces.shape[0])
    def _(k):
        pieces[k] = jnp.zeros(pieces.shape[1:], f32)

    running[0] = jnp.zeros(running.shape[1:], f32)
    for k in range(GROUP):
        stacked[slots + k] = jnp.zeros(stacked.shape[1:], bf16)
    blank = jnp.zeros((columns, LANES), bf16)
    for c in (cell(0, 0), cell(0, EY - 1), cell(EX - 1, 0), cell(EX - 1, EY - 1)):
        field[c] = blank

    def fill(there, ref):
        @pl.when(jnp.logical_not(there))
        def _():
            ref[...] = jnp.zeros(ref.shape, ref.dtype)

    sides = (up, down, left, right)
    fill(up, field.at[pl.ds(cell(0, 1), FY)])
    fill(down, field.at[pl.ds(cell(EX - 1, 1), FY)])
    fill(left, rim_cols.at[0])
    fill(right, rim_cols.at[1])
    fill(up, got_rows.at[0])
    fill(down, got_rows.at[1])
    fill(left, got_cols.at[0])
    fill(right, got_cols.at[1])
    fill(up, got_rows_2.at[0])
    fill(down, got_rows_2.at[1])
    fill(left, got_cols_2.at[0])
    fill(right, got_cols_2.at[1])
    for k in range(4):
        fill(from_diagonals[k], got_diag.at[k])

    for r in range(FX):
        for c in range(FY):
            field[cell(r + 1, c + 1)] = x_ref[r * FY + c]

    vertical = up.astype(jnp.int32) + down.astype(jnp.int32)
    sideways = left.astype(jnp.int32) + right.astype(jnp.int32)
    pl.semaphore_wait(barrier, subs - 1 + slabs - 1 + vertical * sideways)

    def remote(src, dst, send, recv, di, dj):
        return pltpu.make_async_remote_copy(
            src_ref=src, dst_ref=dst, send_sem=send, recv_sem=recv,
            device_id={"sub": di, "slab": dj}, device_id_type=MESH,
        )

    def exchange(copies):
        for there, coming, copy in copies:
            @pl.when(there)
            def _():
                copy.start()

    def arrive(copies):
        for there, coming, copy in copies:
            @pl.when(coming)
            def _():
                copy.wait_recv()

    def leave(copies):
        for there, coming, copy in copies:
            @pl.when(there)
            def _():
                copy.wait_send()

    x_cols = x_ref.reshape(FX, FY, columns, LANES)
    first = (
        (up, down, remote(x_ref.at[pl.ds(0, FY)], field.at[pl.ds(cell(EX - 1, 1), FY)],
                          s0.at[0], r0.at[0], i - 1, j)),
        (down, up, remote(x_ref.at[pl.ds((FX - 1) * FY, FY)], field.at[pl.ds(cell(0, 1), FY)],
                          s0.at[1], r0.at[1], i + 1, j)),
        (left, right, remote(x_cols.at[:, 0], rim_cols.at[1], s0.at[2], r0.at[2], i, j - 1)),
        (right, left, remote(x_cols.at[:, FY - 1], rim_cols.at[0], s0.at[3], r0.at[3], i, j + 1)),
    )
    exchange(first)
    list_copy.wait()
    arrive(first)
    for r in range(FX):
        field[cell(r + 1, 0)] = rim_cols[0, r]
        field[cell(r + 1, EY - 1)] = rim_cols[1, r]

    rows_in = columns * GROUP
    groups = group_count(slots)

    def apply():
        @pl.loop(0, slots // GATHER)
        def _(g):
            for k in range(GATHER):
                e = g * GATHER + k
                x = jnp.concatenate(
                    [field[meta_ref[e, 3 + p]][:, :dofs] for p in range(6)], axis=1
                )
                stacked[e] = x

        @pl.loop(0, groups)
        def _(g):
            start = meta_ref[g, 10]
            x = stacked[pl.ds(start, GROUP)].reshape(rows_in, 6 * dofs)
            y = lax.dot_general(
                x, jac[meta_ref[g, 9]], NT, preferred_element_type=f32
            )
            for k in range(GROUP):
                for p in range(6):
                    pieces[(g * GROUP + k) * 6 + p, :, :dofs] = y[
                        k * columns : (k + 1) * columns, p * dofs : (p + 1) * dofs
                    ]

        def add(n, total):
            for k in range(SUMS):
                at = n * SUMS + k
                total = jnp.where(meta_ref[at, 1] > 0, 0.0, total) + pieces[meta_ref[at, 0]]
                running[1 + at] = total
            return total

        lax.fori_loop(0, 6 * slots // SUMS, add, jnp.zeros((columns, LANES), f32))

        @pl.loop(0, CELLS // SPREAD)
        def _(n):
            for k in range(SPREAD):
                c = n * SPREAD + k
                total = running[meta_ref[c, 2]]
                totals[c] = total
                sent[c] = total.astype(bf16)

    apply()
    for r in range(FX):
        for k in range(2):
            sent_cols[0, r, k] = sent[cell(r + 1, k)]
            sent_cols[1, r, k] = sent[cell(r + 1, FY + k)]
    corners = (
        (cell(FX, EY - 1), cell(EX - 1, FY)),
        (cell(FX, 0), cell(EX - 1, 1)),
        (cell(1, EY - 1), cell(0, FY)),
        (cell(1, 0), cell(0, 1)),
    )
    for k in range(4):
        for n in range(2):
            sent_diag[k, n] = sent[corners[k][n]]
    span = EY + FY
    second = (
        (up, down, remote(sent.at[pl.ds(cell(0, 1), span)], got_rows.at[1],
                          s1.at[0], r1.at[0], i - 1, j)),
        (down, up, remote(sent.at[pl.ds(cell(FX, 1), span)], got_rows.at[0],
                          s1.at[1], r1.at[1], i + 1, j)),
        (left, right, remote(sent_cols.at[0], got_cols.at[1], s1.at[2], r1.at[2], i, j - 1)),
        (right, left, remote(sent_cols.at[1], got_cols.at[0], s1.at[3], r1.at[3], i, j + 1)),
    ) + tuple(
        (diagonals[k][0], from_diagonals[k],
         remote(sent_diag.at[k], got_diag.at[k], s1.at[4 + k], r1.at[4 + k],
                diagonals[k][1], diagonals[k][2]))
        for k in range(4)
    )
    exchange(second)
    leave(first)
    arrive(second)

    def wide(ref, *at):
        return ref[at].astype(f32)

    for r in range(1, FX + 1):
        for c in range(1, FY + 1):
            v = totals[cell(r, c)]
            if r == 1:
                v = v + wide(got_rows, 0, EY + c - 1)
            if r == FX:
                v = v + wide(got_rows, 1, c - 1)
            if c == 1:
                v = v + wide(got_cols, 0, r - 1, 1)
            if c == FY:
                v = v + wide(got_cols, 1, r - 1, 0)
            field[cell(r, c)] = v.astype(bf16)

    def keep(there, c, v):
        field[c] = jnp.where(there, v, 0.0).astype(bf16)

    for c in range(1, FY + 1):
        v = totals[cell(0, c)] + wide(got_rows, 0, c - 1)
        w = totals[cell(EX - 1, c)] + wide(got_rows, 1, EY + c - 1)
        if c == 1:
            v, w = v + wide(got_diag, 0, 0), w + wide(got_diag, 2, 0)
        if c == FY:
            v, w = v + wide(got_diag, 1, 0), w + wide(got_diag, 3, 0)
        keep(up, cell(0, c), v)
        keep(down, cell(EX - 1, c), w)
    for r in range(1, FX + 1):
        v = totals[cell(r, 0)] + wide(got_cols, 0, r - 1, 0)
        w = totals[cell(r, EY - 1)] + wide(got_cols, 1, r - 1, 1)
        if r == 1:
            v, w = v + wide(got_diag, 0, 1), w + wide(got_diag, 1, 1)
        if r == FX:
            v, w = v + wide(got_diag, 2, 1), w + wide(got_diag, 3, 1)
        keep(left, cell(r, 0), v)
        keep(right, cell(r, EY - 1), w)

    own = range(FX * FY)
    local = lax.dot_general(
        jnp.concatenate([x_ref[k] for k in own], axis=1),
        jnp.concatenate([field[cell(k // FY + 1, k % FY + 1)] for k in own], axis=1),
        NT, preferred_element_type=f32,
    )
    local = local * (1.0 / math.sqrt(FX * FY * dofs))
    ids = ids_ref[...]
    width = dense.shape[1]
    spots = lax.broadcasted_iota(jnp.int32, (width, columns), 0)
    one_hot = jnp.where(spots == ids, 1.0, 0.0).astype(f32)
    rows = lax.broadcasted_iota(jnp.int32, (8 * subs, columns), 0)
    spot = jnp.where(rows % 8 < CV, rows // 8 * CV + rows % 8, -1)
    row_hot = jnp.where(spot == ids, 1.0, 0.0).astype(f32)
    placed = lax.dot_general(
        local, one_hot, NT, precision=lax.Precision.HIGHEST, preferred_element_type=f32
    )
    dense[...] = jnp.dot(
        row_hot, placed, precision=lax.Precision.HIGHEST, preferred_element_type=f32
    )

    def block(s):
        return dense.at[pl.ds(pl.multiple_of(s * 8, 8), 8)]

    def to_sub(s):
        return remote(block(s), got_dense.at[i], cs1.at[s], cr1.at[i], s, j)

    def from_sub(s):
        return remote(block(s), got_dense.at[s], cs1.at[s], cr1.at[s], s, j)

    def to_slab(s):
        return remote(row_sum, got_sum.at[j], cs2.at[s], cr2.at[j], i, s)

    def from_slab(s):
        return remote(row_sum, got_sum.at[s], cs2.at[s], cr2.at[s], i, s)

    @pl.loop(1, subs)
    def _(k):
        to_sub(lax.rem(i + k, subs)).start()

    leave(second)
    apply()

    for r in range(FX):
        sent_cols_2[0, r] = sent[cell(r + 1, 0)]
        sent_cols_2[1, r] = sent[cell(r + 1, EY - 1)]
    third = (
        (up, down, remote(sent.at[pl.ds(cell(0, 1), FY)], got_rows_2.at[1],
                          s2.at[0], r2.at[0], i - 1, j)),
        (down, up, remote(sent.at[pl.ds(cell(EX - 1, 1), FY)], got_rows_2.at[0],
                          s2.at[1], r2.at[1], i + 1, j)),
        (left, right, remote(sent_cols_2.at[0], got_cols_2.at[1], s2.at[2], r2.at[2], i, j - 1)),
        (right, left, remote(sent_cols_2.at[1], got_cols_2.at[0], s2.at[3], r2.at[3], i, j + 1)),
    )
    exchange(third)

    row_sum[...] = block(i)[...]

    @pl.loop(1, subs)
    def _(k):
        s = lax.rem(i + k, subs)
        from_sub(s).wait_recv()
        row_sum[...] += got_dense[s]

    @pl.loop(1, slabs)
    def _(k):
        to_slab(lax.rem(j + k, slabs)).start()

    arrive(third)
    for r in range(1, FX + 1):
        for c in range(1, FY + 1):
            v = totals[cell(r, c)]
            if r == 1:
                v = v + wide(got_rows_2, 0, c - 1)
            if r == FX:
                v = v + wide(got_rows_2, 1, c - 1)
            if c == 1:
                v = v + wide(got_cols_2, 0, r - 1)
            if c == FY:
                v = v + wide(got_cols_2, 1, r - 1)
            out_ref[(r - 1) * FY + c - 1] = v.astype(bf16)

    coarse_ref[...] = row_sum[...]

    @pl.loop(1, slabs)
    def _(k):
        s = lax.rem(j + k, slabs)
        from_slab(s).wait_recv()
        coarse_ref[...] += got_sum[s]

    leave(third)

    @pl.loop(1, subs)
    def _(k):
        to_sub(lax.rem(i + k, subs)).wait_send()

    @pl.loop(1, slabs)
    def _(k):
        to_slab(lax.rem(j + k, slabs)).wait_send()


def body(coarse_basis, jacobians, element_faces, element_type, element_count, vertex_ids):
    subs, slabs = lax.axis_size("sub"), lax.axis_size("slab")
    dofs = jacobians.shape[1] // 6
    columns = coarse_basis.shape[2] // dofs
    slots = element_faces.shape[0]
    vertex_total = CV * subs
    width = -(-vertex_total // LANES) * LANES
    f32, bf16 = jnp.float32, jnp.bfloat16

    x = coarse_basis.reshape(FX * FY, dofs, columns).transpose(0, 2, 1)
    x = jnp.pad(x, ((0, 0), (0, 0), (0, LANES - dofs)))
    groups = group_count(slots)

    def block(*lead):
        return pltpu.VMEM((*lead, columns, LANES), bf16)

    vmem = pl.BlockSpec(memory_space=pltpu.VMEM)
    dma = pltpu.SemaphoreType.DMA
    out, coarse = pl.pallas_call(
        functools.partial(kernel, subs, slabs, slots, dofs),
        out_shape=(
            jax.ShapeDtypeStruct((FX * FY, columns, LANES), bf16),
            jax.ShapeDtypeStruct((8, width), f32),
        ),
        in_specs=[
            vmem,
            vmem,
            vmem,
            vmem,
            pl.BlockSpec(memory_space=pltpu.SMEM),
            vmem,
        ],
        out_specs=(vmem, vmem),
        scratch_shapes=[
            block(CELLS),
            pltpu.VMEM((6 * slots, LANES), jnp.int32),
            pltpu.SMEM((6 * slots, LANES), jnp.int32),
            pltpu.VMEM((slots + GROUP, columns, 6 * dofs), bf16),
            pltpu.VMEM((6 * GROUP * groups, columns, LANES), f32),
            pltpu.VMEM((1 + 6 * slots, columns, LANES), f32),
            pltpu.VMEM((CELLS, columns, LANES), f32),
            block(CELLS),
            block(2, FX, 2),
            block(4, 2),
            block(2, FX),
            block(2, FX),
            block(2, EY + FY),
            block(2, FX, 2),
            block(4, 2),
            block(2, FY),
            block(2, FX),
            pltpu.VMEM((8 * subs, width), f32),
            pltpu.VMEM((subs, 8, width), f32),
            pltpu.VMEM((8, width), f32),
            pltpu.VMEM((slabs, 8, width), f32),
            dma,
            dma((4,)), dma((4,)),
            dma((8,)), dma((8,)),
            dma((4,)), dma((4,)),
            dma((subs,)), dma((subs,)),
            dma((slabs,)), dma((slabs,)),
        ],
        compiler_params=pltpu.CompilerParams(
            collective_id=0, has_side_effects=True, vmem_limit_bytes=40 * 1024 * 1024
        ),
        cost_estimate=pl.CostEstimate(
            flops=4 * slots * (6 * dofs) ** 2 * columns,
            bytes_accessed=2 * jacobians.size,
            transcendentals=0,
        ),
    )(x, jacobians, element_faces.T, element_type.reshape(1, slots), element_count, vertex_ids)
    out = out[:, :, :dofs].transpose(0, 2, 1).reshape(FX, FY, dofs * columns)
    return out, coarse[:CV, :vertex_total]


def solution(mesh):
    return jax.shard_map(
        body,
        mesh=mesh,
        in_specs=(
            P("sub", "slab", None),
            P(),
            P(("sub", "slab"), None),
            P(("sub", "slab")),
            P(("sub", "slab")),
            P(("sub", "slab"), None),
        ),
        out_specs=(P("sub", "slab", None), P("sub", None)),
        check_vma=False,
    )
```

```python
import functools
import math

import jax
import jax.numpy as jnp
from jax import lax
from jax.experimental import pallas as pl
from jax.experimental.pallas import tpu as pltpu
from jax.sharding import PartitionSpec as P

FX = 4
FY = 8
EX = FX + 2
EY = FY + 2
CELLS = EX * EY
CV = 4
TYPES = 4
LANES = 128
GROUP = 4
GATHER = 4
TOGETHER = 2
SUMS = 8
SPREAD = 4
MESH = pl.DeviceIdType.MESH
NT = (((1,), (1,)), ((), ()))


def cell(r, c):
    return r * EY + c


def group_count(slots):
    return (slots + TYPES * (GROUP - 1)) // GROUP


def index_lists(faces_ref, kinds_ref, count, lists):
    slots, groups = faces_ref.shape[1], group_count(faces_ref.shape[1])
    i32 = jnp.int32

    def iota(rows, cols, axis):
        return lax.broadcasted_iota(i32, (rows, cols), axis)

    def count_of(mask, axis):
        return jnp.sum(jnp.where(mask, 1, 0), axis=axis, keepdims=True)

    def as_column(row):
        n = row.shape[1]
        return jnp.sum(jnp.where(iota(n, n, 0) == iota(n, n, 1), row, 0), axis=1, keepdims=True)

    def put(lane, column):
        lists[pl.ds(0, column.shape[0]), lane : lane + 1] = column

    lists[...] = jnp.zeros(lists.shape, i32)
    live = iota(1, slots, 1) < count
    kind = jnp.where(live, kinds_ref[...], TYPES)
    kind_col = as_column(kind)
    earlier = iota(slots, slots, 0) < iota(slots, slots, 1)
    in_kind = count_of((kind_col == kind) & earlier, 0)
    place = in_kind + count_of(kind_col < kind, 0)
    group = iota(groups, 1, 0)
    group_type = jnp.zeros((groups, 1), i32)
    group_start = jnp.zeros((groups, 1), i32)
    position = in_kind
    first_group = jnp.zeros((1, 1), i32)
    first_place = jnp.zeros((1, 1), i32)
    for t in range(TYPES):
        number = count_of(kind == t, 1)
        needed = lax.shift_right_logical(number + (GROUP - 1), 2)
        inside = (group >= first_group) & (group < first_group + needed)
        group_type = jnp.where(inside, t, group_type)
        group_start = jnp.where(inside, first_place + GROUP * (group - first_group), group_start)
        position = position + jnp.where(kind == t, GROUP * first_group, 0)
        first_group = first_group + needed
        first_place = first_place + number
    faces = [faces_ref[p : p + 1, :] for p in range(6)]
    cells = jnp.concatenate([jnp.where(live, f, CELLS) for f in faces], axis=1)
    piece = jnp.concatenate([position * 6 + p for p in range(6)], axis=1)
    total = 6 * slots
    cells_col = as_column(cells)
    before = iota(total, total, 0) < iota(total, total, 1)
    in_cell = count_of((cells_col == cells) & before, 0)
    rank = in_cell + count_of(cells_col < cells, 0)
    chosen = rank == iota(total, 1, 0)
    put(0, jnp.sum(jnp.where(chosen, piece, 0), axis=1, keepdims=True))
    put(1, jnp.sum(jnp.where(chosen, jnp.where(in_cell == 0, 1, 0), 0), axis=1, keepdims=True))
    spot = iota(CELLS, 1, 0)
    upto = count_of(cells <= spot, 1)
    put(2, jnp.where(count_of(cells == spot, 1) > 0, upto, 0))
    taken = place == iota(slots, 1, 0)
    for p in range(6):
        put(3 + p, jnp.sum(jnp.where(taken, faces[p], 0), axis=1, keepdims=True))
    put(9, group_type)
    put(10, group_start)


def kernel(
    subs, slabs, slots, dofs,
    x_ref, jac_ref, faces_ref, kinds_ref, count_ref, ids_ref,
    out_ref, coarse_ref,
    field, lists, meta_ref, jac, stacked, pieces, running, totals, sent, sent_cols, sent_diag, sent_cols_2,
    rim_cols, got_rows, got_cols, got_diag, got_rows_2, got_cols_2,
    dense, got_dense, row_sum, got_sum,
    list_sem, s0, r0, s1, r1, s2, r2, cs1, cr1, cs2, cr2,
):
    i = lax.axis_index("sub")
    j = lax.axis_index("slab")
    up, down, left, right = i > 0, i < subs - 1, j > 0, j < slabs - 1
    columns = x_ref.shape[1]
    f32 = jnp.float32
    bf16 = jnp.bfloat16

    barrier = pltpu.get_barrier_semaphore()

    def greet(di, dj):
        pl.semaphore_signal(barrier, inc=1, device_id={"sub": di, "slab": dj}, device_id_type=MESH)

    diagonals = (
        (jnp.logical_and(down, right), i + 1, j + 1),
        (jnp.logical_and(down, left), i + 1, j - 1),
        (jnp.logical_and(up, right), i - 1, j + 1),
        (jnp.logical_and(up, left), i - 1, j - 1),
    )
    from_diagonals = tuple(diagonals[3 - k][0] for k in range(4))

    @pl.loop(1, subs)
    def _(k):
        greet(lax.rem(i + k, subs), j)

    @pl.loop(1, slabs)
    def _(k):
        greet(i, lax.rem(j + k, slabs))

    for there, di, dj in diagonals:
        @pl.when(there)
        def _():
            greet(di, dj)

    index_lists(faces_ref, kinds_ref, count_ref[0], lists)
    list_copy = pltpu.make_async_copy(lists, meta_ref, list_sem)
    list_copy.start()

    running[0] = jnp.zeros(running.shape[1:], f32)
    for k in range(GROUP):
        stacked[slots + k] = jnp.zeros(stacked.shape[1:], bf16)
    blank = jnp.zeros((columns, LANES), bf16)
    for c in (cell(0, 0), cell(0, EY - 1), cell(EX - 1, 0), cell(EX - 1, EY - 1)):
        field[c] = blank

    def fill(there, ref):
        @pl.when(jnp.logical_not(there))
        def _():
            ref[...] = jnp.zeros(ref.shape, ref.dtype)

    sides = (up, down, left, right)
    fill(up, field.at[pl.ds(cell(0, 1), FY)])
    fill(down, field.at[pl.ds(cell(EX - 1, 1), FY)])
    fill(left, rim_cols.at[0])
    fill(right, rim_cols.at[1])
    fill(up, got_rows.at[0])
    fill(down, got_rows.at[1])
    fill(left, got_cols.at[0])
    fill(right, got_cols.at[1])
    fill(up, got_rows_2.at[0])
    fill(down, got_rows_2.at[1])
    fill(left, got_cols_2.at[0])
    fill(right, got_cols_2.at[1])
    for k in range(4):
        fill(from_diagonals[k], got_diag.at[k])

    for r in range(FX):
        for c in range(FY):
            field[cell(r + 1, c + 1)] = x_ref[r * FY + c]

    vertical = up.astype(jnp.int32) + down.astype(jnp.int32)
    sideways = left.astype(jnp.int32) + right.astype(jnp.int32)
    pl.semaphore_wait(barrier, subs - 1 + slabs - 1 + vertical * sideways)

    def remote(src, dst, send, recv, di, dj):
        return pltpu.make_async_remote_copy(
            src_ref=src, dst_ref=dst, send_sem=send, recv_sem=recv,
            device_id={"sub": di, "slab": dj}, device_id_type=MESH,
        )

    def exchange(copies):
        for there, coming, copy in copies:
            @pl.when(there)
            def _():
                copy.start()

    def arrive(copies):
        for there, coming, copy in copies:
            @pl.when(coming)
            def _():
                copy.wait_recv()

    def leave(copies):
        for there, coming, copy in copies:
            @pl.when(there)
            def _():
                copy.wait_send()

    x_cols = x_ref.reshape(FX, FY, columns, LANES)
    first = (
        (up, down, remote(x_ref.at[pl.ds(0, FY)], field.at[pl.ds(cell(EX - 1, 1), FY)],
                          s0.at[0], r0.at[0], i - 1, j)),
        (down, up, remote(x_ref.at[pl.ds((FX - 1) * FY, FY)], field.at[pl.ds(cell(0, 1), FY)],
                          s0.at[1], r0.at[1], i + 1, j)),
        (left, right, remote(x_cols.at[:, 0], rim_cols.at[1], s0.at[2], r0.at[2], i, j - 1)),
        (right, left, remote(x_cols.at[:, FY - 1], rim_cols.at[0], s0.at[3], r0.at[3], i, j + 1)),
    )
    exchange(first)

    @pl.loop(0, TYPES * 6)
    def _(n):
        t, r = n // 6, n % 6
        top = pl.multiple_of(r * LANES, LANES)
        face_rows = jac_ref[t, r]
        end = jnp.zeros((dofs, LANES - dofs), bf16)
        for p in range(6):
            lanes = slice(p * LANES, (p + 1) * LANES)
            jac[t, pl.ds(top + LANES - 16, 16), lanes] = jnp.zeros((16, LANES), bf16)
            jac[t, pl.ds(top, dofs), lanes] = jnp.concatenate(
                [face_rows[:, p * dofs : (p + 1) * dofs], end], axis=1
            )

    list_copy.wait()
    arrive(first)
    for r in range(FX):
        field[cell(r + 1, 0)] = rim_cols[0, r]
        field[cell(r + 1, EY - 1)] = rim_cols[1, r]

    rows_in = columns * GROUP
    groups = group_count(slots)

    def apply():
        @pl.loop(0, slots // GATHER)
        def _(g):
            for k in range(GATHER):
                e = g * GATHER + k
                for p in range(6):
                    stacked[e, :, p * LANES : (p + 1) * LANES] = field[meta_ref[e, 3 + p]]

        @pl.loop(0, groups // TOGETHER)
        def _(n):
            for m in range(TOGETHER):
                g = n * TOGETHER + m
                x = stacked[pl.ds(meta_ref[g, 10], GROUP)].reshape(rows_in, 6 * LANES)
                y = lax.dot_general(x, jac[meta_ref[g, 9]], NT, preferred_element_type=f32)
                for k in range(GROUP):
                    for p in range(6):
                        pieces[(g * GROUP + k) * 6 + p] = y[
                            k * columns : (k + 1) * columns, p * LANES : (p + 1) * LANES
                        ]

        def add(n, total):
            for k in range(SUMS):
                at = n * SUMS + k
                total = jnp.where(meta_ref[at, 1] > 0, 0.0, total) + pieces[meta_ref[at, 0]]
                running[1 + at] = total
            return total

        lax.fori_loop(0, 6 * slots // SUMS, add, jnp.zeros((columns, LANES), f32))

        @pl.loop(0, CELLS // SPREAD)
        def _(n):
            for k in range(SPREAD):
                c = n * SPREAD + k
                total = running[meta_ref[c, 2]]
                totals[c] = total
                sent[c] = total.astype(bf16)

    apply()
    for r in range(FX):
        for k in range(2):
            sent_cols[0, r, k] = sent[cell(r + 1, k)]
            sent_cols[1, r, k] = sent[cell(r + 1, FY + k)]
    corners = (
        (cell(FX, EY - 1), cell(EX - 1, FY)),
        (cell(FX, 0), cell(EX - 1, 1)),
        (cell(1, EY - 1), cell(0, FY)),
        (cell(1, 0), cell(0, 1)),
    )
    for k in range(4):
        for n in range(2):
            sent_diag[k, n] = sent[corners[k][n]]
    span = EY + FY
    second = (
        (up, down, remote(sent.at[pl.ds(cell(0, 1), span)], got_rows.at[1],
                          s1.at[0], r1.at[0], i - 1, j)),
        (down, up, remote(sent.at[pl.ds(cell(FX, 1), span)], got_rows.at[0],
                          s1.at[1], r1.at[1], i + 1, j)),
        (left, right, remote(sent_cols.at[0], got_cols.at[1], s1.at[2], r1.at[2], i, j - 1)),
        (right, left, remote(sent_cols.at[1], got_cols.at[0], s1.at[3], r1.at[3], i, j + 1)),
    ) + tuple(
        (diagonals[k][0], from_diagonals[k],
         remote(sent_diag.at[k], got_diag.at[k], s1.at[4 + k], r1.at[4 + k],
                diagonals[k][1], diagonals[k][2]))
        for k in range(4)
    )
    exchange(second)
    leave(first)
    arrive(second)

    def wide(ref, *at):
        return ref[at].astype(f32)

    for r in range(1, FX + 1):
        for c in range(1, FY + 1):
            v = totals[cell(r, c)]
            if r == 1:
                v = v + wide(got_rows, 0, EY + c - 1)
            if r == FX:
                v = v + wide(got_rows, 1, c - 1)
            if c == 1:
                v = v + wide(got_cols, 0, r - 1, 1)
            if c == FY:
                v = v + wide(got_cols, 1, r - 1, 0)
            field[cell(r, c)] = v.astype(bf16)

    def keep(there, c, v):
        field[c] = jnp.where(there, v, 0.0).astype(bf16)

    for c in range(1, FY + 1):
        v = totals[cell(0, c)] + wide(got_rows, 0, c - 1)
        w = totals[cell(EX - 1, c)] + wide(got_rows, 1, EY + c - 1)
        if c == 1:
            v, w = v + wide(got_diag, 0, 0), w + wide(got_diag, 2, 0)
        if c == FY:
            v, w = v + wide(got_diag, 1, 0), w + wide(got_diag, 3, 0)
        keep(up, cell(0, c), v)
        keep(down, cell(EX - 1, c), w)
    for r in range(1, FX + 1):
        v = totals[cell(r, 0)] + wide(got_cols, 0, r - 1, 0)
        w = totals[cell(r, EY - 1)] + wide(got_cols, 1, r - 1, 1)
        if r == 1:
            v, w = v + wide(got_diag, 0, 1), w + wide(got_diag, 1, 1)
        if r == FX:
            v, w = v + wide(got_diag, 2, 1), w + wide(got_diag, 3, 1)
        keep(left, cell(r, 0), v)
        keep(right, cell(r, EY - 1), w)

    own = range(FX * FY)
    local = lax.dot_general(
        jnp.concatenate([x_ref[k] for k in own], axis=1),
        jnp.concatenate([field[cell(k // FY + 1, k % FY + 1)] for k in own], axis=1),
        NT, preferred_element_type=f32,
    )
    local = local * (1.0 / math.sqrt(FX * FY * dofs))
    ids = ids_ref[...]
    width = dense.shape[1]
    spots = lax.broadcasted_iota(jnp.int32, (width, columns), 0)
    one_hot = jnp.where(spots == ids, 1.0, 0.0).astype(f32)
    rows = lax.broadcasted_iota(jnp.int32, (8 * subs, columns), 0)
    spot = jnp.where(rows % 8 < CV, rows // 8 * CV + rows % 8, -1)
    row_hot = jnp.where(spot == ids, 1.0, 0.0).astype(f32)
    placed = lax.dot_general(
        local, one_hot, NT, precision=lax.Precision.HIGHEST, preferred_element_type=f32
    )
    dense[...] = jnp.dot(
        row_hot, placed, precision=lax.Precision.HIGHEST, preferred_element_type=f32
    )

    def block(s):
        return dense.at[pl.ds(pl.multiple_of(s * 8, 8), 8)]

    def to_sub(s):
        return remote(block(s), got_dense.at[i], cs1.at[s], cr1.at[i], s, j)

    def from_sub(s):
        return remote(block(s), got_dense.at[s], cs1.at[s], cr1.at[s], s, j)

    def to_slab(s):
        return remote(row_sum, got_sum.at[j], cs2.at[s], cr2.at[j], i, s)

    def from_slab(s):
        return remote(row_sum, got_sum.at[s], cs2.at[s], cr2.at[s], i, s)

    @pl.loop(1, subs)
    def _(k):
        to_sub(lax.rem(i + k, subs)).start()

    leave(second)
    apply()

    for r in range(FX):
        sent_cols_2[0, r] = sent[cell(r + 1, 0)]
        sent_cols_2[1, r] = sent[cell(r + 1, EY - 1)]
    third = (
        (up, down, remote(sent.at[pl.ds(cell(0, 1), FY)], got_rows_2.at[1],
                          s2.at[0], r2.at[0], i - 1, j)),
        (down, up, remote(sent.at[pl.ds(cell(EX - 1, 1), FY)], got_rows_2.at[0],
                          s2.at[1], r2.at[1], i + 1, j)),
        (left, right, remote(sent_cols_2.at[0], got_cols_2.at[1], s2.at[2], r2.at[2], i, j - 1)),
        (right, left, remote(sent_cols_2.at[1], got_cols_2.at[0], s2.at[3], r2.at[3], i, j + 1)),
    )
    exchange(third)

    row_sum[...] = block(i)[...]

    @pl.loop(1, subs)
    def _(k):
        s = lax.rem(i + k, subs)
        from_sub(s).wait_recv()
        row_sum[...] += got_dense[s]

    @pl.loop(1, slabs)
    def _(k):
        to_slab(lax.rem(j + k, slabs)).start()

    arrive(third)
    for r in range(1, FX + 1):
        for c in range(1, FY + 1):
            v = totals[cell(r, c)]
            if r == 1:
                v = v + wide(got_rows_2, 0, c - 1)
            if r == FX:
                v = v + wide(got_rows_2, 1, c - 1)
            if c == 1:
                v = v + wide(got_cols_2, 0, r - 1)
            if c == FY:
                v = v + wide(got_cols_2, 1, r - 1)
            out_ref[(r - 1) * FY + c - 1] = v.astype(bf16)

    coarse_ref[...] = row_sum[...]

    @pl.loop(1, slabs)
    def _(k):
        s = lax.rem(j + k, slabs)
        from_slab(s).wait_recv()
        coarse_ref[...] += got_sum[s]

    leave(third)

    @pl.loop(1, subs)
    def _(k):
        to_sub(lax.rem(i + k, subs)).wait_send()

    @pl.loop(1, slabs)
    def _(k):
        to_slab(lax.rem(j + k, slabs)).wait_send()


def body(coarse_basis, jacobians, element_faces, element_type, element_count, vertex_ids):
    subs, slabs = lax.axis_size("sub"), lax.axis_size("slab")
    dofs = jacobians.shape[1] // 6
    columns = coarse_basis.shape[2] // dofs
    slots = element_faces.shape[0]
    vertex_total = CV * subs
    width = -(-vertex_total // LANES) * LANES
    f32, bf16 = jnp.float32, jnp.bfloat16

    x = coarse_basis.reshape(FX * FY, dofs, columns).transpose(0, 2, 1)
    x = jnp.pad(x, ((0, 0), (0, 0), (0, LANES - dofs)))
    groups = group_count(slots)
    jac = jacobians.reshape(TYPES, 6, dofs, 6 * dofs)

    def block(*lead):
        return pltpu.VMEM((*lead, columns, LANES), bf16)

    vmem = pl.BlockSpec(memory_space=pltpu.VMEM)
    dma = pltpu.SemaphoreType.DMA
    out, coarse = pl.pallas_call(
        functools.partial(kernel, subs, slabs, slots, dofs),
        out_shape=(
            jax.ShapeDtypeStruct((FX * FY, columns, LANES), bf16),
            jax.ShapeDtypeStruct((8, width), f32),
        ),
        in_specs=[
            vmem,
            vmem,
            vmem,
            vmem,
            pl.BlockSpec(memory_space=pltpu.SMEM),
            vmem,
        ],
        out_specs=(vmem, vmem),
        scratch_shapes=[
            block(CELLS),
            pltpu.VMEM((6 * slots, LANES), jnp.int32),
            pltpu.SMEM((6 * slots, LANES), jnp.int32),
            pltpu.VMEM((TYPES, 6 * LANES, 6 * LANES), bf16),
            pltpu.VMEM((slots + GROUP, columns, 6 * LANES), bf16),
            pltpu.VMEM((6 * GROUP * groups, columns, LANES), f32),
            pltpu.VMEM((1 + 6 * slots, columns, LANES), f32),
            pltpu.VMEM((CELLS, columns, LANES), f32),
            block(CELLS),
            block(2, FX, 2),
            block(4, 2),
            block(2, FX),
            block(2, FX),
            block(2, EY + FY),
            block(2, FX, 2),
            block(4, 2),
            block(2, FY),
            block(2, FX),
            pltpu.VMEM((8 * subs, width), f32),
            pltpu.VMEM((subs, 8, width), f32),
            pltpu.VMEM((8, width), f32),
            pltpu.VMEM((slabs, 8, width), f32),
            dma,
            dma((4,)), dma((4,)),
            dma((8,)), dma((8,)),
            dma((4,)), dma((4,)),
            dma((subs,)), dma((subs,)),
            dma((slabs,)), dma((slabs,)),
        ],
        compiler_params=pltpu.CompilerParams(
            collective_id=0, has_side_effects=True, vmem_limit_bytes=40 * 1024 * 1024
        ),
        cost_estimate=pl.CostEstimate(
            flops=4 * slots * (6 * dofs) ** 2 * columns,
            bytes_accessed=2 * jacobians.size,
            transcendentals=0,
        ),
    )(x, jac, element_faces.T, element_type.reshape(1, slots), element_count, vertex_ids)
    out = out[:, :, :dofs].transpose(0, 2, 1).reshape(FX, FY, dofs * columns)
    return out, coarse[:CV, :vertex_total]


def solution(mesh):
    return jax.shard_map(
        body,
        mesh=mesh,
        in_specs=(
            P("sub", "slab", None),
            P(),
            P(("sub", "slab"), None),
            P(("sub", "slab")),
            P(("sub", "slab")),
            P(("sub", "slab"), None),
        ),
        out_specs=(P("sub", "slab", None), P("sub", None)),
        check_vma=False,
    )
```

```python
import functools
import math

import jax
import jax.numpy as jnp
from jax import lax
from jax.experimental import pallas as pl
from jax.experimental.pallas import tpu as pltpu
from jax.sharding import PartitionSpec as P

FX = 4
FY = 8
EX = FX + 2
EY = FY + 2
CELLS = EX * EY
CV = 4
TYPES = 4
LANES = 128
GROUP = 4
GATHER = 4
TOGETHER = 4
SUMS = 8
SPREAD = 4
MESH = pl.DeviceIdType.MESH
NT = (((1,), (1,)), ((), ()))


def cell(r, c):
    return r * EY + c


def group_count(slots):
    return (slots + TYPES * (GROUP - 1)) // GROUP


def index_lists(faces_ref, kinds_ref, count, lists):
    slots, groups = faces_ref.shape[1], group_count(faces_ref.shape[1])
    i32 = jnp.int32

    def iota(rows, cols, axis):
        return lax.broadcasted_iota(i32, (rows, cols), axis)

    def count_of(mask, axis):
        return jnp.sum(jnp.where(mask, 1, 0), axis=axis, keepdims=True)

    def as_column(row):
        n = row.shape[1]
        return jnp.sum(jnp.where(iota(n, n, 0) == iota(n, n, 1), row, 0), axis=1, keepdims=True)

    def put(lane, column):
        lists[pl.ds(0, column.shape[0]), lane : lane + 1] = column

    lists[...] = jnp.zeros(lists.shape, i32)
    live = iota(1, slots, 1) < count
    kind = jnp.where(live, kinds_ref[...], TYPES)
    kind_col = as_column(kind)
    earlier = iota(slots, slots, 0) < iota(slots, slots, 1)
    in_kind = count_of((kind_col == kind) & earlier, 0)
    place = in_kind + count_of(kind_col < kind, 0)
    group = iota(groups, 1, 0)
    group_type = jnp.zeros((groups, 1), i32)
    group_start = jnp.zeros((groups, 1), i32)
    position = in_kind
    first_group = jnp.zeros((1, 1), i32)
    first_place = jnp.zeros((1, 1), i32)
    for t in range(TYPES):
        number = count_of(kind == t, 1)
        needed = lax.shift_right_logical(number + (GROUP - 1), 2)
        inside = (group >= first_group) & (group < first_group + needed)
        group_type = jnp.where(inside, t, group_type)
        group_start = jnp.where(inside, first_place + GROUP * (group - first_group), group_start)
        position = position + jnp.where(kind == t, GROUP * first_group, 0)
        first_group = first_group + needed
        first_place = first_place + number
    faces = [faces_ref[p : p + 1, :] for p in range(6)]
    cells = jnp.concatenate([jnp.where(live, f, CELLS) for f in faces], axis=1)
    piece = jnp.concatenate([position * 6 + p for p in range(6)], axis=1)
    total = 6 * slots
    cells_col = as_column(cells)
    before = iota(total, total, 0) < iota(total, total, 1)
    in_cell = count_of((cells_col == cells) & before, 0)
    rank = in_cell + count_of(cells_col < cells, 0)
    chosen = rank == iota(total, 1, 0)
    put(0, jnp.sum(jnp.where(chosen, piece, 0), axis=1, keepdims=True))
    put(1, jnp.sum(jnp.where(chosen, jnp.where(in_cell == 0, 1, 0), 0), axis=1, keepdims=True))
    spot = iota(CELLS, 1, 0)
    upto = count_of(cells <= spot, 1)
    put(2, jnp.where(count_of(cells == spot, 1) > 0, upto, 0))
    taken = place == iota(slots, 1, 0)
    for p in range(6):
        put(3 + p, jnp.sum(jnp.where(taken, faces[p], 0), axis=1, keepdims=True))
    put(9, group_type)
    put(10, group_start)


def two_parts(x, axis):
    high = x.astype(jnp.bfloat16)
    rest = (x - high.astype(jnp.float32)).astype(jnp.bfloat16)
    return jnp.concatenate([high, rest], axis=axis)


def kernel(
    subs, slabs, slots, dofs,
    x_ref, jac_ref, faces_ref, kinds_ref, count_ref, ids_ref,
    out_ref, coarse_ref,
    field, lists, meta_ref, jac, stacked, pieces, running, totals, sent, sent_cols, sent_diag, sent_cols_2,
    rim_cols, got_rows, got_cols, got_diag, got_rows_2, got_cols_2,
    one_hot, row_hot, dense, got_dense, row_sum, got_sum,
    list_sem, s0, r0, s1, r1, s2, r2, cs1, cr1, cs2, cr2,
):
    i = lax.axis_index("sub")
    j = lax.axis_index("slab")
    up, down, left, right = i > 0, i < subs - 1, j > 0, j < slabs - 1
    columns = x_ref.shape[1]
    f32 = jnp.float32
    bf16 = jnp.bfloat16

    barrier = pltpu.get_barrier_semaphore()

    def greet(di, dj):
        pl.semaphore_signal(barrier, inc=1, device_id={"sub": di, "slab": dj}, device_id_type=MESH)

    diagonals = (
        (jnp.logical_and(down, right), i + 1, j + 1),
        (jnp.logical_and(down, left), i + 1, j - 1),
        (jnp.logical_and(up, right), i - 1, j + 1),
        (jnp.logical_and(up, left), i - 1, j - 1),
    )
    from_diagonals = tuple(diagonals[3 - k][0] for k in range(4))

    @pl.loop(1, subs)
    def _(k):
        greet(lax.rem(i + k, subs), j)

    @pl.loop(1, slabs)
    def _(k):
        greet(i, lax.rem(j + k, slabs))

    for there, di, dj in diagonals:
        @pl.when(there)
        def _():
            greet(di, dj)

    index_lists(faces_ref, kinds_ref, count_ref[0], lists)
    list_copy = pltpu.make_async_copy(lists, meta_ref, list_sem)
    list_copy.start()

    ids = jnp.concatenate([ids_ref[...]] * 2, axis=1)
    spots = lax.broadcasted_iota(jnp.int32, one_hot.shape, 0)
    one_hot[...] = jnp.where(spots == ids, 1.0, 0.0).astype(bf16)
    rows = lax.broadcasted_iota(jnp.int32, row_hot.shape, 0)
    spot = jnp.where(rows % 8 < CV, rows // 8 * CV + rows % 8, -1)
    row_hot[...] = jnp.where(spot == ids, 1.0, 0.0).astype(bf16)

    running[0] = jnp.zeros(running.shape[1:], f32)
    for k in range(GROUP):
        stacked[slots + k] = jnp.zeros(stacked.shape[1:], bf16)
    blank = jnp.zeros((columns, LANES), bf16)
    for c in (cell(0, 0), cell(0, EY - 1), cell(EX - 1, 0), cell(EX - 1, EY - 1)):
        field[c] = blank

    def fill(there, ref):
        @pl.when(jnp.logical_not(there))
        def _():
            ref[...] = jnp.zeros(ref.shape, ref.dtype)

    sides = (up, down, left, right)
    fill(up, field.at[pl.ds(cell(0, 1), FY)])
    fill(down, field.at[pl.ds(cell(EX - 1, 1), FY)])
    fill(left, rim_cols.at[0])
    fill(right, rim_cols.at[1])
    fill(up, got_rows.at[0])
    fill(down, got_rows.at[1])
    fill(left, got_cols.at[0])
    fill(right, got_cols.at[1])
    fill(up, got_rows_2.at[0])
    fill(down, got_rows_2.at[1])
    fill(left, got_cols_2.at[0])
    fill(right, got_cols_2.at[1])
    for k in range(4):
        fill(from_diagonals[k], got_diag.at[k])

    for r in range(FX):
        for c in range(FY):
            field[cell(r + 1, c + 1)] = x_ref[r * FY + c]

    vertical = up.astype(jnp.int32) + down.astype(jnp.int32)
    sideways = left.astype(jnp.int32) + right.astype(jnp.int32)
    pl.semaphore_wait(barrier, subs - 1 + slabs - 1 + vertical * sideways)

    def remote(src, dst, send, recv, di, dj):
        return pltpu.make_async_remote_copy(
            src_ref=src, dst_ref=dst, send_sem=send, recv_sem=recv,
            device_id={"sub": di, "slab": dj}, device_id_type=MESH,
        )

    def exchange(copies):
        for there, coming, copy in copies:
            @pl.when(there)
            def _():
                copy.start()

    def arrive(copies):
        for there, coming, copy in copies:
            @pl.when(coming)
            def _():
                copy.wait_recv()

    def leave(copies):
        for there, coming, copy in copies:
            @pl.when(there)
            def _():
                copy.wait_send()

    x_cols = x_ref.reshape(FX, FY, columns, LANES)
    first = (
        (up, down, remote(x_ref.at[pl.ds(0, FY)], field.at[pl.ds(cell(EX - 1, 1), FY)],
                          s0.at[0], r0.at[0], i - 1, j)),
        (down, up, remote(x_ref.at[pl.ds((FX - 1) * FY, FY)], field.at[pl.ds(cell(0, 1), FY)],
                          s0.at[1], r0.at[1], i + 1, j)),
        (left, right, remote(x_cols.at[:, 0], rim_cols.at[1], s0.at[2], r0.at[2], i, j - 1)),
        (right, left, remote(x_cols.at[:, FY - 1], rim_cols.at[0], s0.at[3], r0.at[3], i, j + 1)),
    )
    exchange(first)

    @pl.loop(0, TYPES * 6)
    def _(n):
        t, r = n // 6, n % 6
        top = pl.multiple_of(r * LANES, LANES)
        face_rows = jac_ref[t, r]
        end = jnp.zeros((dofs, LANES - dofs), bf16)
        for p in range(6):
            lanes = slice(p * LANES, (p + 1) * LANES)
            jac[t, pl.ds(top + LANES - 16, 16), lanes] = jnp.zeros((16, LANES), bf16)
            jac[t, pl.ds(top, dofs), lanes] = jnp.concatenate(
                [face_rows[:, p * dofs : (p + 1) * dofs], end], axis=1
            )

    list_copy.wait()
    arrive(first)
    for r in range(FX):
        field[cell(r + 1, 0)] = rim_cols[0, r]
        field[cell(r + 1, EY - 1)] = rim_cols[1, r]

    rows_in = columns * GROUP
    groups = group_count(slots)

    def apply():
        @pl.loop(0, slots // GATHER)
        def _(g):
            for k in range(GATHER):
                e = g * GATHER + k
                for p in range(6):
                    stacked[e, :, p * LANES : (p + 1) * LANES] = field[meta_ref[e, 3 + p]]

        @pl.loop(0, groups // TOGETHER)
        def _(n):
            for m in range(TOGETHER):
                g = n * TOGETHER + m
                x = stacked[pl.ds(meta_ref[g, 10], GROUP)].reshape(rows_in, 6 * LANES)
                y = lax.dot_general(x, jac[meta_ref[g, 9]], NT, preferred_element_type=f32)
                for k in range(GROUP):
                    for p in range(6):
                        pieces[(g * GROUP + k) * 6 + p] = y[
                            k * columns : (k + 1) * columns, p * LANES : (p + 1) * LANES
                        ]

        def add(n, total):
            for k in range(SUMS):
                at = n * SUMS + k
                total = jnp.where(meta_ref[at, 1] > 0, 0.0, total) + pieces[meta_ref[at, 0]]
                running[1 + at] = total
            return total

        lax.fori_loop(0, 6 * slots // SUMS, add, jnp.zeros((columns, LANES), f32))

        @pl.loop(0, CELLS // SPREAD)
        def _(n):
            for k in range(SPREAD):
                c = n * SPREAD + k
                total = running[meta_ref[c, 2]]
                totals[c] = total
                sent[c] = total.astype(bf16)

    apply()
    for r in range(FX):
        for k in range(2):
            sent_cols[0, r, k] = sent[cell(r + 1, k)]
            sent_cols[1, r, k] = sent[cell(r + 1, FY + k)]
    corners = (
        (cell(FX, EY - 1), cell(EX - 1, FY)),
        (cell(FX, 0), cell(EX - 1, 1)),
        (cell(1, EY - 1), cell(0, FY)),
        (cell(1, 0), cell(0, 1)),
    )
    for k in range(4):
        for n in range(2):
            sent_diag[k, n] = sent[corners[k][n]]
    span = EY + FY
    second = (
        (up, down, remote(sent.at[pl.ds(cell(0, 1), span)], got_rows.at[1],
                          s1.at[0], r1.at[0], i - 1, j)),
        (down, up, remote(sent.at[pl.ds(cell(FX, 1), span)], got_rows.at[0],
                          s1.at[1], r1.at[1], i + 1, j)),
        (left, right, remote(sent_cols.at[0], got_cols.at[1], s1.at[2], r1.at[2], i, j - 1)),
        (right, left, remote(sent_cols.at[1], got_cols.at[0], s1.at[3], r1.at[3], i, j + 1)),
    ) + tuple(
        (diagonals[k][0], from_diagonals[k],
         remote(sent_diag.at[k], got_diag.at[k], s1.at[4 + k], r1.at[4 + k],
                diagonals[k][1], diagonals[k][2]))
        for k in range(4)
    )
    exchange(second)
    leave(first)
    arrive(second)

    def wide(ref, *at):
        return ref[at].astype(f32)

    for r in range(1, FX + 1):
        for c in range(1, FY + 1):
            v = totals[cell(r, c)]
            if r == 1:
                v = v + wide(got_rows, 0, EY + c - 1)
            if r == FX:
                v = v + wide(got_rows, 1, c - 1)
            if c == 1:
                v = v + wide(got_cols, 0, r - 1, 1)
            if c == FY:
                v = v + wide(got_cols, 1, r - 1, 0)
            field[cell(r, c)] = v.astype(bf16)

    def keep(there, c, v):
        field[c] = jnp.where(there, v, 0.0).astype(bf16)

    for c in range(1, FY + 1):
        v = totals[cell(0, c)] + wide(got_rows, 0, c - 1)
        w = totals[cell(EX - 1, c)] + wide(got_rows, 1, EY + c - 1)
        if c == 1:
            v, w = v + wide(got_diag, 0, 0), w + wide(got_diag, 2, 0)
        if c == FY:
            v, w = v + wide(got_diag, 1, 0), w + wide(got_diag, 3, 0)
        keep(up, cell(0, c), v)
        keep(down, cell(EX - 1, c), w)
    for r in range(1, FX + 1):
        v = totals[cell(r, 0)] + wide(got_cols, 0, r - 1, 0)
        w = totals[cell(r, EY - 1)] + wide(got_cols, 1, r - 1, 1)
        if r == 1:
            v, w = v + wide(got_diag, 0, 1), w + wide(got_diag, 1, 1)
        if r == FX:
            v, w = v + wide(got_diag, 2, 1), w + wide(got_diag, 3, 1)
        keep(left, cell(r, 0), v)
        keep(right, cell(r, EY - 1), w)

    own = range(FX * FY)
    local = lax.dot_general(
        jnp.concatenate([x_ref[k] for k in own], axis=1),
        jnp.concatenate([field[cell(k // FY + 1, k % FY + 1)] for k in own], axis=1),
        NT, preferred_element_type=f32,
    )
    local = local * (1.0 / math.sqrt(FX * FY * dofs))
    placed = lax.dot_general(
        two_parts(local, 1), one_hot[...], NT, preferred_element_type=f32
    )
    dense[...] = jnp.dot(row_hot[...], two_parts(placed, 0), preferred_element_type=f32)

    def block(s):
        return dense.at[pl.ds(pl.multiple_of(s * 8, 8), 8)]

    def to_sub(s):
        return remote(block(s), got_dense.at[i], cs1.at[s], cr1.at[i], s, j)

    def from_sub(s):
        return remote(block(s), got_dense.at[s], cs1.at[s], cr1.at[s], s, j)

    def to_slab(s):
        return remote(row_sum, got_sum.at[j], cs2.at[s], cr2.at[j], i, s)

    def from_slab(s):
        return remote(row_sum, got_sum.at[s], cs2.at[s], cr2.at[s], i, s)

    @pl.loop(1, subs)
    def _(k):
        to_sub(lax.rem(i + k, subs)).start()

    leave(second)
    apply()

    for r in range(FX):
        sent_cols_2[0, r] = sent[cell(r + 1, 0)]
        sent_cols_2[1, r] = sent[cell(r + 1, EY - 1)]
    third = (
        (up, down, remote(sent.at[pl.ds(cell(0, 1), FY)], got_rows_2.at[1],
                          s2.at[0], r2.at[0], i - 1, j)),
        (down, up, remote(sent.at[pl.ds(cell(EX - 1, 1), FY)], got_rows_2.at[0],
                          s2.at[1], r2.at[1], i + 1, j)),
        (left, right, remote(sent_cols_2.at[0], got_cols_2.at[1], s2.at[2], r2.at[2], i, j - 1)),
        (right, left, remote(sent_cols_2.at[1], got_cols_2.at[0], s2.at[3], r2.at[3], i, j + 1)),
    )
    exchange(third)

    row_sum[...] = block(i)[...]

    @pl.loop(1, subs)
    def _(k):
        s = lax.rem(i + k, subs)
        from_sub(s).wait_recv()
        row_sum[...] += got_dense[s]

    @pl.loop(1, slabs)
    def _(k):
        to_slab(lax.rem(j + k, slabs)).start()

    arrive(third)
    for r in range(1, FX + 1):
        for c in range(1, FY + 1):
            v = totals[cell(r, c)]
            if r == 1:
                v = v + wide(got_rows_2, 0, c - 1)
            if r == FX:
                v = v + wide(got_rows_2, 1, c - 1)
            if c == 1:
                v = v + wide(got_cols_2, 0, r - 1)
            if c == FY:
                v = v + wide(got_cols_2, 1, r - 1)
            out_ref[(r - 1) * FY + c - 1] = v.astype(bf16)

    coarse_ref[...] = row_sum[...]

    @pl.loop(1, slabs)
    def _(k):
        s = lax.rem(j + k, slabs)
        from_slab(s).wait_recv()
        coarse_ref[...] += got_sum[s]

    leave(third)

    @pl.loop(1, subs)
    def _(k):
        to_sub(lax.rem(i + k, subs)).wait_send()

    @pl.loop(1, slabs)
    def _(k):
        to_slab(lax.rem(j + k, slabs)).wait_send()


def body(coarse_basis, jacobians, element_faces, element_type, element_count, vertex_ids):
    subs, slabs = lax.axis_size("sub"), lax.axis_size("slab")
    dofs = jacobians.shape[1] // 6
    columns = coarse_basis.shape[2] // dofs
    slots = element_faces.shape[0]
    vertex_total = CV * subs
    width = -(-vertex_total // LANES) * LANES
    f32, bf16 = jnp.float32, jnp.bfloat16

    x = coarse_basis.reshape(FX * FY, dofs, columns).transpose(0, 2, 1)
    x = jnp.pad(x, ((0, 0), (0, 0), (0, LANES - dofs)))
    groups = group_count(slots)
    jac = jacobians.reshape(TYPES, 6, dofs, 6 * dofs)

    def block(*lead):
        return pltpu.VMEM((*lead, columns, LANES), bf16)

    vmem = pl.BlockSpec(memory_space=pltpu.VMEM)
    dma = pltpu.SemaphoreType.DMA
    out, coarse = pl.pallas_call(
        functools.partial(kernel, subs, slabs, slots, dofs),
        out_shape=(
            jax.ShapeDtypeStruct((FX * FY, columns, LANES), bf16),
            jax.ShapeDtypeStruct((8, width), f32),
        ),
        in_specs=[
            vmem,
            vmem,
            vmem,
            vmem,
            pl.BlockSpec(memory_space=pltpu.SMEM),
            vmem,
        ],
        out_specs=(vmem, vmem),
        scratch_shapes=[
            block(CELLS),
            pltpu.VMEM((6 * slots, LANES), jnp.int32),
            pltpu.SMEM((6 * slots, LANES), jnp.int32),
            pltpu.VMEM((TYPES, 6 * LANES, 6 * LANES), bf16),
            pltpu.VMEM((slots + GROUP, columns, 6 * LANES), bf16),
            pltpu.VMEM((6 * GROUP * groups, columns, LANES), f32),
            pltpu.VMEM((1 + 6 * slots, columns, LANES), f32),
            pltpu.VMEM((CELLS, columns, LANES), f32),
            block(CELLS),
            block(2, FX, 2),
            block(4, 2),
            block(2, FX),
            block(2, FX),
            block(2, EY + FY),
            block(2, FX, 2),
            block(4, 2),
            block(2, FY),
            block(2, FX),
            pltpu.VMEM((width, 2 * columns), bf16),
            pltpu.VMEM((8 * subs, 2 * columns), bf16),
            pltpu.VMEM((8 * subs, width), f32),
            pltpu.VMEM((subs, 8, width), f32),
            pltpu.VMEM((8, width), f32),
            pltpu.VMEM((slabs, 8, width), f32),
            dma,
            dma((4,)), dma((4,)),
            dma((8,)), dma((8,)),
            dma((4,)), dma((4,)),
            dma((subs,)), dma((subs,)),
            dma((slabs,)), dma((slabs,)),
        ],
        compiler_params=pltpu.CompilerParams(
            collective_id=0, has_side_effects=True, vmem_limit_bytes=40 * 1024 * 1024
        ),
        cost_estimate=pl.CostEstimate(
            flops=4 * slots * (6 * dofs) ** 2 * columns,
            bytes_accessed=2 * jacobians.size,
            transcendentals=0,
        ),
    )(x, jac, element_faces.T, element_type.reshape(1, slots), element_count, vertex_ids)
    out = out[:, :, :dofs].transpose(0, 2, 1).reshape(FX, FY, dofs * columns)
    return out, coarse[:CV, :vertex_total]


def solution(mesh):
    return jax.shard_map(
        body,
        mesh=mesh,
        in_specs=(
            P("sub", "slab", None),
            P(),
            P(("sub", "slab"), None),
            P(("sub", "slab")),
            P(("sub", "slab")),
            P(("sub", "slab"), None),
        ),
        out_specs=(P("sub", "slab", None), P("sub", None)),
        check_vma=False,
    )
```

```python
import functools
import math

import jax
import jax.numpy as jnp
from jax import lax
from jax.experimental import pallas as pl
from jax.experimental.pallas import tpu as pltpu
from jax.sharding import PartitionSpec as P

FX = 4
FY = 8
EX = FX + 2
EY = FY + 2
CELLS = EX * EY
CV = 4
TYPES = 4
LANES = 128
GROUP = 4
GATHER = 4
TOGETHER = 4
SUMS = 8
SPREAD = 4
MESH = pl.DeviceIdType.MESH
NT = (((1,), (1,)), ((), ()))


def cell(r, c):
    return r * EY + c


def group_count(slots):
    return (slots + TYPES * (GROUP - 1)) // GROUP


def index_lists(faces_ref, kinds_ref, count, lists):
    slots, groups = faces_ref.shape[1], group_count(faces_ref.shape[1])
    i32 = jnp.int32

    def iota(rows, cols, axis):
        return lax.broadcasted_iota(i32, (rows, cols), axis)

    def count_of(mask, axis):
        return jnp.sum(jnp.where(mask, 1, 0), axis=axis, keepdims=True)

    def as_column(row):
        n = row.shape[1]
        return jnp.sum(jnp.where(iota(n, n, 0) == iota(n, n, 1), row, 0), axis=1, keepdims=True)

    def put(lane, column):
        lists[pl.ds(0, column.shape[0]), lane : lane + 1] = column

    lists[...] = jnp.zeros(lists.shape, i32)
    live = iota(1, slots, 1) < count
    kind = jnp.where(live, kinds_ref[...], TYPES)
    kind_col = as_column(kind)
    earlier = iota(slots, slots, 0) < iota(slots, slots, 1)
    in_kind = count_of((kind_col == kind) & earlier, 0)
    place = in_kind + count_of(kind_col < kind, 0)
    group = iota(groups, 1, 0)
    group_type = jnp.zeros((groups, 1), i32)
    group_start = jnp.zeros((groups, 1), i32)
    position = in_kind
    first_group = jnp.zeros((1, 1), i32)
    first_place = jnp.zeros((1, 1), i32)
    for t in range(TYPES):
        number = count_of(kind == t, 1)
        needed = lax.shift_right_logical(number + (GROUP - 1), 2)
        inside = (group >= first_group) & (group < first_group + needed)
        group_type = jnp.where(inside, t, group_type)
        group_start = jnp.where(inside, first_place + GROUP * (group - first_group), group_start)
        position = position + jnp.where(kind == t, GROUP * first_group, 0)
        first_group = first_group + needed
        first_place = first_place + number
    faces = [faces_ref[p : p + 1, :] for p in range(6)]
    cells = jnp.concatenate([jnp.where(live, f, CELLS) for f in faces], axis=1)
    piece = jnp.concatenate([position * 6 + p for p in range(6)], axis=1)
    total = 6 * slots
    cells_col = as_column(cells)
    before = iota(total, total, 0) < iota(total, total, 1)
    in_cell = count_of((cells_col == cells) & before, 0)
    rank = in_cell + count_of(cells_col < cells, 0)
    chosen = rank == iota(total, 1, 0)
    put(0, jnp.sum(jnp.where(chosen, piece, 0), axis=1, keepdims=True))
    put(1, jnp.sum(jnp.where(chosen, jnp.where(in_cell == 0, 1, 0), 0), axis=1, keepdims=True))
    spot = iota(CELLS, 1, 0)
    upto = count_of(cells <= spot, 1)
    put(2, jnp.where(count_of(cells == spot, 1) > 0, upto, 0))
    taken = place == iota(slots, 1, 0)
    for p in range(6):
        put(3 + p, jnp.sum(jnp.where(taken, faces[p], 0), axis=1, keepdims=True))
    put(9, group_type)
    put(10, group_start)


def two_parts(x, axis):
    high = x.astype(jnp.bfloat16)
    rest = (x - high.astype(jnp.float32)).astype(jnp.bfloat16)
    return jnp.concatenate([high, rest], axis=axis)


def columns_first(basis_ref, turned, flat):
    f32 = jnp.float32
    cells, columns = FX * FY, flat.shape[0] // (FX * FY)
    length = basis_ref.shape[2]
    per = LANES // columns
    parts = LANES // cells
    steps = LANES // (per * parts)
    for n in range(steps):
        blocks = []
        for q in range(parts):
            low = (q * steps + n) * LANES
            high = min(low + LANES, length)
            block = jnp.concatenate(
                [basis_ref[r, :, low:high].astype(f32) for r in range(FX)], axis=0
            )
            if high - low < LANES:
                end = jnp.zeros((cells, LANES - (high - low)), f32)
                block = jnp.concatenate([block, end], axis=1)
            blocks.append(block)
        turned[n * LANES : (n + 1) * LANES, :] = jnp.concatenate(blocks, axis=0).T
    for n in range(columns // per):
        rows = [turned[pl.ds(n * per + k, LANES // per, stride=columns), :] for k in range(per)]
        block = jnp.concatenate(rows, axis=0).T
        for k in range(per):
            lanes = slice(k * (LANES // per), (k + 1) * (LANES // per))
            flat[pl.ds(n * per + k, cells, stride=columns), :] = jnp.concatenate(
                [block[q * cells : (q + 1) * cells, lanes] for q in range(parts)], axis=1
            )


def dofs_first(flat, turned, out_ref):
    cells, columns = FX * FY, flat.shape[0] // (FX * FY)
    length = out_ref.shape[2]
    per = LANES // columns
    parts = LANES // cells
    steps = LANES // (per * parts)
    span = LANES // parts
    for n in range(columns // per):
        rows = [flat[pl.ds(n * per + k, cells, stride=columns), :] for k in range(per)]
        block = jnp.concatenate(
            [
                jnp.concatenate([row[:, q * span : (q + 1) * span] for row in rows], axis=1)
                for q in range(parts)
            ],
            axis=0,
        ).T
        for k in range(per):
            turned[pl.ds(n * per + k, LANES // per, stride=columns), :] = block[
                k * (LANES // per) : (k + 1) * (LANES // per)
            ]
    for n in range(steps):
        block = turned[n * LANES : (n + 1) * LANES, :].T
        for q in range(parts):
            low = (q * steps + n) * LANES
            high = min(low + LANES, length)
            for r in range(FX):
                top = q * cells + r * FY
                out_ref[r, :, low:high] = block[top : top + FY, : high - low].astype(out_ref.dtype)


def kernel(
    subs, slabs, slots, dofs,
    basis_ref, jac_ref, faces_ref, kinds_ref, count_ref, ids_ref,
    out_ref, coarse_ref,
    x_ref, turned, flat, field, lists, meta_ref, jac, stacked, pieces, running, totals, sent, sent_cols, sent_diag, sent_cols_2,
    rim_cols, got_rows, got_cols, got_diag, got_rows_2, got_cols_2,
    one_hot, row_hot, dense, got_dense, row_sum, got_sum,
    list_sem, s0, r0, s1, r1, s2, r2, cs1, cr1, cs2, cr2,
):
    i = lax.axis_index("sub")
    j = lax.axis_index("slab")
    up, down, left, right = i > 0, i < subs - 1, j > 0, j < slabs - 1
    columns = x_ref.shape[1]
    f32 = jnp.float32
    bf16 = jnp.bfloat16

    barrier = pltpu.get_barrier_semaphore()

    def greet(di, dj):
        pl.semaphore_signal(barrier, inc=1, device_id={"sub": di, "slab": dj}, device_id_type=MESH)

    diagonals = (
        (jnp.logical_and(down, right), i + 1, j + 1),
        (jnp.logical_and(down, left), i + 1, j - 1),
        (jnp.logical_and(up, right), i - 1, j + 1),
        (jnp.logical_and(up, left), i - 1, j - 1),
    )
    from_diagonals = tuple(diagonals[3 - k][0] for k in range(4))

    @pl.loop(1, subs)
    def _(k):
        greet(lax.rem(i + k, subs), j)

    @pl.loop(1, slabs)
    def _(k):
        greet(i, lax.rem(j + k, slabs))

    for there, di, dj in diagonals:
        @pl.when(there)
        def _():
            greet(di, dj)

    index_lists(faces_ref, kinds_ref, count_ref[0], lists)
    list_copy = pltpu.make_async_copy(lists, meta_ref, list_sem)
    list_copy.start()

    ids = jnp.concatenate([ids_ref[...]] * 2, axis=1)
    spots = lax.broadcasted_iota(jnp.int32, one_hot.shape, 0)
    one_hot[...] = jnp.where(spots == ids, 1.0, 0.0).astype(bf16)
    rows = lax.broadcasted_iota(jnp.int32, row_hot.shape, 0)
    spot = jnp.where(rows % 8 < CV, rows // 8 * CV + rows % 8, -1)
    row_hot[...] = jnp.where(spot == ids, 1.0, 0.0).astype(bf16)

    running[0] = jnp.zeros(running.shape[1:], f32)
    for k in range(GROUP):
        stacked[slots + k] = jnp.zeros(stacked.shape[1:], bf16)
    blank = jnp.zeros((columns, LANES), bf16)
    for c in (cell(0, 0), cell(0, EY - 1), cell(EX - 1, 0), cell(EX - 1, EY - 1)):
        field[c] = blank

    def fill(there, ref):
        @pl.when(jnp.logical_not(there))
        def _():
            ref[...] = jnp.zeros(ref.shape, ref.dtype)

    sides = (up, down, left, right)
    fill(up, field.at[pl.ds(cell(0, 1), FY)])
    fill(down, field.at[pl.ds(cell(EX - 1, 1), FY)])
    fill(left, rim_cols.at[0])
    fill(right, rim_cols.at[1])
    fill(up, got_rows.at[0])
    fill(down, got_rows.at[1])
    fill(left, got_cols.at[0])
    fill(right, got_cols.at[1])
    fill(up, got_rows_2.at[0])
    fill(down, got_rows_2.at[1])
    fill(left, got_cols_2.at[0])
    fill(right, got_cols_2.at[1])
    for k in range(4):
        fill(from_diagonals[k], got_diag.at[k])

    columns_first(basis_ref, turned, flat)
    for r in range(FX):
        for c in range(FY):
            k = r * FY + c
            block = flat[k * columns : (k + 1) * columns, :].astype(bf16)
            x_ref[k] = block
            field[cell(r + 1, c + 1)] = block

    vertical = up.astype(jnp.int32) + down.astype(jnp.int32)
    sideways = left.astype(jnp.int32) + right.astype(jnp.int32)
    pl.semaphore_wait(barrier, subs - 1 + slabs - 1 + vertical * sideways)

    def remote(src, dst, send, recv, di, dj):
        return pltpu.make_async_remote_copy(
            src_ref=src, dst_ref=dst, send_sem=send, recv_sem=recv,
            device_id={"sub": di, "slab": dj}, device_id_type=MESH,
        )

    def exchange(copies):
        for there, coming, copy in copies:
            @pl.when(there)
            def _():
                copy.start()

    def arrive(copies):
        for there, coming, copy in copies:
            @pl.when(coming)
            def _():
                copy.wait_recv()

    def leave(copies):
        for there, coming, copy in copies:
            @pl.when(there)
            def _():
                copy.wait_send()

    x_cols = x_ref.reshape(FX, FY, columns, LANES)
    first = (
        (up, down, remote(x_ref.at[pl.ds(0, FY)], field.at[pl.ds(cell(EX - 1, 1), FY)],
                          s0.at[0], r0.at[0], i - 1, j)),
        (down, up, remote(x_ref.at[pl.ds((FX - 1) * FY, FY)], field.at[pl.ds(cell(0, 1), FY)],
                          s0.at[1], r0.at[1], i + 1, j)),
        (left, right, remote(x_cols.at[:, 0], rim_cols.at[1], s0.at[2], r0.at[2], i, j - 1)),
        (right, left, remote(x_cols.at[:, FY - 1], rim_cols.at[0], s0.at[3], r0.at[3], i, j + 1)),
    )
    exchange(first)

    @pl.loop(0, TYPES * 6)
    def _(n):
        t, r = n // 6, n % 6
        top = pl.multiple_of(r * LANES, LANES)
        face_rows = jac_ref[t, r]
        end = jnp.zeros((dofs, LANES - dofs), bf16)
        for p in range(6):
            lanes = slice(p * LANES, (p + 1) * LANES)
            jac[t, pl.ds(top + LANES - 16, 16), lanes] = jnp.zeros((16, LANES), bf16)
            jac[t, pl.ds(top, dofs), lanes] = jnp.concatenate(
                [face_rows[:, p * dofs : (p + 1) * dofs], end], axis=1
            )

    list_copy.wait()
    arrive(first)
    for r in range(FX):
        field[cell(r + 1, 0)] = rim_cols[0, r]
        field[cell(r + 1, EY - 1)] = rim_cols[1, r]

    rows_in = columns * GROUP
    groups = group_count(slots)

    def apply():
        @pl.loop(0, slots // GATHER)
        def _(g):
            for k in range(GATHER):
                e = g * GATHER + k
                for p in range(6):
                    stacked[e, :, p * LANES : (p + 1) * LANES] = field[meta_ref[e, 3 + p]]

        @pl.loop(0, groups // TOGETHER)
        def _(n):
            for m in range(TOGETHER):
                g = n * TOGETHER + m
                x = stacked[pl.ds(meta_ref[g, 10], GROUP)].reshape(rows_in, 6 * LANES)
                y = lax.dot_general(x, jac[meta_ref[g, 9]], NT, preferred_element_type=f32)
                for k in range(GROUP):
                    for p in range(6):
                        pieces[(g * GROUP + k) * 6 + p] = y[
                            k * columns : (k + 1) * columns, p * LANES : (p + 1) * LANES
                        ]

        def add(n, total):
            for k in range(SUMS):
                at = n * SUMS + k
                total = jnp.where(meta_ref[at, 1] > 0, 0.0, total) + pieces[meta_ref[at, 0]]
                running[1 + at] = total
            return total

        lax.fori_loop(0, 6 * slots // SUMS, add, jnp.zeros((columns, LANES), f32))

        @pl.loop(0, CELLS // SPREAD)
        def _(n):
            for k in range(SPREAD):
                c = n * SPREAD + k
                total = running[meta_ref[c, 2]]
                totals[c] = total
                sent[c] = total.astype(bf16)

    apply()
    for r in range(FX):
        for k in range(2):
            sent_cols[0, r, k] = sent[cell(r + 1, k)]
            sent_cols[1, r, k] = sent[cell(r + 1, FY + k)]
    corners = (
        (cell(FX, EY - 1), cell(EX - 1, FY)),
        (cell(FX, 0), cell(EX - 1, 1)),
        (cell(1, EY - 1), cell(0, FY)),
        (cell(1, 0), cell(0, 1)),
    )
    for k in range(4):
        for n in range(2):
            sent_diag[k, n] = sent[corners[k][n]]
    span = EY + FY
    second = (
        (up, down, remote(sent.at[pl.ds(cell(0, 1), span)], got_rows.at[1],
                          s1.at[0], r1.at[0], i - 1, j)),
        (down, up, remote(sent.at[pl.ds(cell(FX, 1), span)], got_rows.at[0],
                          s1.at[1], r1.at[1], i + 1, j)),
        (left, right, remote(sent_cols.at[0], got_cols.at[1], s1.at[2], r1.at[2], i, j - 1)),
        (right, left, remote(sent_cols.at[1], got_cols.at[0], s1.at[3], r1.at[3], i, j + 1)),
    ) + tuple(
        (diagonals[k][0], from_diagonals[k],
         remote(sent_diag.at[k], got_diag.at[k], s1.at[4 + k], r1.at[4 + k],
                diagonals[k][1], diagonals[k][2]))
        for k in range(4)
    )
    exchange(second)
    leave(first)
    arrive(second)

    def wide(ref, *at):
        return ref[at].astype(f32)

    for r in range(1, FX + 1):
        for c in range(1, FY + 1):
            v = totals[cell(r, c)]
            if r == 1:
                v = v + wide(got_rows, 0, EY + c - 1)
            if r == FX:
                v = v + wide(got_rows, 1, c - 1)
            if c == 1:
                v = v + wide(got_cols, 0, r - 1, 1)
            if c == FY:
                v = v + wide(got_cols, 1, r - 1, 0)
            field[cell(r, c)] = v.astype(bf16)

    def keep(there, c, v):
        field[c] = jnp.where(there, v, 0.0).astype(bf16)

    for c in range(1, FY + 1):
        v = totals[cell(0, c)] + wide(got_rows, 0, c - 1)
        w = totals[cell(EX - 1, c)] + wide(got_rows, 1, EY + c - 1)
        if c == 1:
            v, w = v + wide(got_diag, 0, 0), w + wide(got_diag, 2, 0)
        if c == FY:
            v, w = v + wide(got_diag, 1, 0), w + wide(got_diag, 3, 0)
        keep(up, cell(0, c), v)
        keep(down, cell(EX - 1, c), w)
    for r in range(1, FX + 1):
        v = totals[cell(r, 0)] + wide(got_cols, 0, r - 1, 0)
        w = totals[cell(r, EY - 1)] + wide(got_cols, 1, r - 1, 1)
        if r == 1:
            v, w = v + wide(got_diag, 0, 1), w + wide(got_diag, 1, 1)
        if r == FX:
            v, w = v + wide(got_diag, 2, 1), w + wide(got_diag, 3, 1)
        keep(left, cell(r, 0), v)
        keep(right, cell(r, EY - 1), w)

    own = range(FX * FY)
    local = lax.dot_general(
        jnp.concatenate([x_ref[k] for k in own], axis=1),
        jnp.concatenate([field[cell(k // FY + 1, k % FY + 1)] for k in own], axis=1),
        NT, preferred_element_type=f32,
    )
    local = local * (1.0 / math.sqrt(FX * FY * dofs))
    placed = lax.dot_general(
        two_parts(local, 1), one_hot[...], NT, preferred_element_type=f32
    )
    dense[...] = jnp.dot(row_hot[...], two_parts(placed, 0), preferred_element_type=f32)

    def block(s):
        return dense.at[pl.ds(pl.multiple_of(s * 8, 8), 8)]

    def to_sub(s):
        return remote(block(s), got_dense.at[i], cs1.at[s], cr1.at[i], s, j)

    def from_sub(s):
        return remote(block(s), got_dense.at[s], cs1.at[s], cr1.at[s], s, j)

    def to_slab(s):
        return remote(row_sum, got_sum.at[j], cs2.at[s], cr2.at[j], i, s)

    def from_slab(s):
        return remote(row_sum, got_sum.at[s], cs2.at[s], cr2.at[s], i, s)

    @pl.loop(1, subs)
    def _(k):
        to_sub(lax.rem(i + k, subs)).start()

    leave(second)
    apply()

    for r in range(FX):
        sent_cols_2[0, r] = sent[cell(r + 1, 0)]
        sent_cols_2[1, r] = sent[cell(r + 1, EY - 1)]
    third = (
        (up, down, remote(sent.at[pl.ds(cell(0, 1), FY)], got_rows_2.at[1],
                          s2.at[0], r2.at[0], i - 1, j)),
        (down, up, remote(sent.at[pl.ds(cell(EX - 1, 1), FY)], got_rows_2.at[0],
                          s2.at[1], r2.at[1], i + 1, j)),
        (left, right, remote(sent_cols_2.at[0], got_cols_2.at[1], s2.at[2], r2.at[2], i, j - 1)),
        (right, left, remote(sent_cols_2.at[1], got_cols_2.at[0], s2.at[3], r2.at[3], i, j + 1)),
    )
    exchange(third)

    row_sum[...] = block(i)[...]

    @pl.loop(1, subs)
    def _(k):
        s = lax.rem(i + k, subs)
        from_sub(s).wait_recv()
        row_sum[...] += got_dense[s]

    @pl.loop(1, slabs)
    def _(k):
        to_slab(lax.rem(j + k, slabs)).start()

    arrive(third)
    for r in range(1, FX + 1):
        for c in range(1, FY + 1):
            v = totals[cell(r, c)]
            if r == 1:
                v = v + wide(got_rows_2, 0, c - 1)
            if r == FX:
                v = v + wide(got_rows_2, 1, c - 1)
            if c == 1:
                v = v + wide(got_cols_2, 0, r - 1)
            if c == FY:
                v = v + wide(got_cols_2, 1, r - 1)
            top = ((r - 1) * FY + c - 1) * columns
            flat[top : top + columns, :] = v
    dofs_first(flat, turned, out_ref)

    coarse_ref[...] = row_sum[...]

    @pl.loop(1, slabs)
    def _(k):
        s = lax.rem(j + k, slabs)
        from_slab(s).wait_recv()
        coarse_ref[...] += got_sum[s]

    leave(third)

    @pl.loop(1, subs)
    def _(k):
        to_sub(lax.rem(i + k, subs)).wait_send()

    @pl.loop(1, slabs)
    def _(k):
        to_slab(lax.rem(j + k, slabs)).wait_send()


def body(coarse_basis, jacobians, element_faces, element_type, element_count, vertex_ids):
    subs, slabs = lax.axis_size("sub"), lax.axis_size("slab")
    dofs = jacobians.shape[1] // 6
    columns = coarse_basis.shape[2] // dofs
    slots = element_faces.shape[0]
    vertex_total = CV * subs
    width = -(-vertex_total // LANES) * LANES
    f32, bf16 = jnp.float32, jnp.bfloat16

    groups = group_count(slots)
    jac = jacobians.reshape(TYPES, 6, dofs, 6 * dofs)

    def block(*lead):
        return pltpu.VMEM((*lead, columns, LANES), bf16)

    vmem = pl.BlockSpec(memory_space=pltpu.VMEM)
    dma = pltpu.SemaphoreType.DMA
    out, coarse = pl.pallas_call(
        functools.partial(kernel, subs, slabs, slots, dofs),
        out_shape=(
            jax.ShapeDtypeStruct(coarse_basis.shape, bf16),
            jax.ShapeDtypeStruct((8, width), f32),
        ),
        in_specs=[
            vmem,
            vmem,
            vmem,
            vmem,
            pl.BlockSpec(memory_space=pltpu.SMEM),
            vmem,
        ],
        out_specs=(vmem, vmem),
        scratch_shapes=[
            block(FX * FY),
            pltpu.VMEM((columns * LANES // (LANES // (FX * FY)), LANES), f32),
            pltpu.VMEM((FX * FY * columns, LANES), f32),
            block(CELLS),
            pltpu.VMEM((6 * slots, LANES), jnp.int32),
            pltpu.SMEM((6 * slots, LANES), jnp.int32),
            pltpu.VMEM((TYPES, 6 * LANES, 6 * LANES), bf16),
            pltpu.VMEM((slots + GROUP, columns, 6 * LANES), bf16),
            pltpu.VMEM((6 * GROUP * groups, columns, LANES), f32),
            pltpu.VMEM((1 + 6 * slots, columns, LANES), f32),
            pltpu.VMEM((CELLS, columns, LANES), f32),
            block(CELLS),
            block(2, FX, 2),
            block(4, 2),
            block(2, FX),
            block(2, FX),
            block(2, EY + FY),
            block(2, FX, 2),
            block(4, 2),
            block(2, FY),
            block(2, FX),
            pltpu.VMEM((width, 2 * columns), bf16),
            pltpu.VMEM((8 * subs, 2 * columns), bf16),
            pltpu.VMEM((8 * subs, width), f32),
            pltpu.VMEM((subs, 8, width), f32),
            pltpu.VMEM((8, width), f32),
            pltpu.VMEM((slabs, 8, width), f32),
            dma,
            dma((4,)), dma((4,)),
            dma((8,)), dma((8,)),
            dma((4,)), dma((4,)),
            dma((subs,)), dma((subs,)),
            dma((slabs,)), dma((slabs,)),
        ],
        compiler_params=pltpu.CompilerParams(
            collective_id=0, has_side_effects=True, vmem_limit_bytes=40 * 1024 * 1024
        ),
        cost_estimate=pl.CostEstimate(
            flops=4 * slots * (6 * dofs) ** 2 * columns,
            bytes_accessed=2 * jacobians.size,
            transcendentals=0,
        ),
    )(coarse_basis, jac, element_faces.T, element_type.reshape(1, slots), element_count, vertex_ids)
    return out, coarse[:CV, :vertex_total]


def solution(mesh):
    return jax.shard_map(
        body,
        mesh=mesh,
        in_specs=(
            P("sub", "slab", None),
            P(),
            P(("sub", "slab"), None),
            P(("sub", "slab")),
            P(("sub", "slab")),
            P(("sub", "slab"), None),
        ),
        out_specs=(P("sub", "slab", None), P("sub", None)),
        check_vma=False,
    )
```

```python
import functools
import math

import jax
import jax.numpy as jnp
from jax import lax
from jax.experimental import pallas as pl
from jax.experimental.pallas import tpu as pltpu
from jax.sharding import PartitionSpec as P

FX = 4
FY = 8
EX = FX + 2
EY = FY + 2
CELLS = EX * EY
CV = 4
TYPES = 4
LANES = 128
GROUP = 4
GATHER = 4
TOGETHER = 4
SUMS = 8
SPREAD = 4
MESH = pl.DeviceIdType.MESH
NT = (((1,), (1,)), ((), ()))


def cell(r, c):
    return r * EY + c


def group_count(slots):
    return (slots + TYPES * (GROUP - 1)) // GROUP


def index_lists(faces_ref, kinds_ref, count, lists):
    slots, groups = faces_ref.shape[1], group_count(faces_ref.shape[1])
    i32 = jnp.int32

    def iota(rows, cols, axis):
        return lax.broadcasted_iota(i32, (rows, cols), axis)

    def count_of(mask, axis):
        return jnp.sum(jnp.where(mask, 1, 0), axis=axis, keepdims=True)

    def as_column(row):
        n = row.shape[1]
        return jnp.sum(jnp.where(iota(n, n, 0) == iota(n, n, 1), row, 0), axis=1, keepdims=True)

    def put(lane, column):
        lists[pl.ds(0, column.shape[0]), lane : lane + 1] = column

    lists[...] = jnp.zeros(lists.shape, i32)
    live = iota(1, slots, 1) < count
    kind = jnp.where(live, kinds_ref[...], TYPES)
    kind_col = as_column(kind)
    earlier = iota(slots, slots, 0) < iota(slots, slots, 1)
    in_kind = count_of((kind_col == kind) & earlier, 0)
    place = in_kind + count_of(kind_col < kind, 0)
    group = iota(groups, 1, 0)
    group_type = jnp.zeros((groups, 1), i32)
    group_start = jnp.zeros((groups, 1), i32)
    position = in_kind
    first_group = jnp.zeros((1, 1), i32)
    first_place = jnp.zeros((1, 1), i32)
    for t in range(TYPES):
        number = count_of(kind == t, 1)
        needed = lax.shift_right_logical(number + (GROUP - 1), 2)
        inside = (group >= first_group) & (group < first_group + needed)
        group_type = jnp.where(inside, t, group_type)
        group_start = jnp.where(inside, first_place + GROUP * (group - first_group), group_start)
        position = position + jnp.where(kind == t, GROUP * first_group, 0)
        first_group = first_group + needed
        first_place = first_place + number
    faces = [faces_ref[p : p + 1, :] for p in range(6)]
    cells = jnp.concatenate([jnp.where(live, f, CELLS) for f in faces], axis=1)
    piece = jnp.concatenate([position * 6 + p for p in range(6)], axis=1)
    total = 6 * slots
    cells_col = as_column(cells)
    before = iota(total, total, 0) < iota(total, total, 1)
    in_cell = count_of((cells_col == cells) & before, 0)
    rank = in_cell + count_of(cells_col < cells, 0)
    chosen = rank == iota(total, 1, 0)
    put(0, jnp.sum(jnp.where(chosen, piece, 0), axis=1, keepdims=True))
    put(1, jnp.sum(jnp.where(chosen, jnp.where(in_cell == 0, 1, 0), 0), axis=1, keepdims=True))
    spot = iota(CELLS, 1, 0)
    upto = count_of(cells <= spot, 1)
    put(2, jnp.where(count_of(cells == spot, 1) > 0, upto, 0))
    taken = place == iota(slots, 1, 0)
    for p in range(6):
        put(3 + p, jnp.sum(jnp.where(taken, faces[p], 0), axis=1, keepdims=True))
    put(9, group_type)
    put(10, group_start)


def two_parts(x, axis):
    high = x.astype(jnp.bfloat16)
    rest = (x - high.astype(jnp.float32)).astype(jnp.bfloat16)
    return jnp.concatenate([high, rest], axis=axis)


def columns_first(basis_ref, turned, flat):
    f32 = jnp.float32
    cells, columns = FX * FY, flat.shape[0] // (FX * FY)
    length = basis_ref.shape[2]
    per = LANES // columns
    parts = LANES // cells
    steps = LANES // (per * parts)
    for n in range(steps):
        blocks = []
        for q in range(parts):
            low = (q * steps + n) * LANES
            high = min(low + LANES, length)
            block = jnp.concatenate(
                [basis_ref[r, :, low:high].astype(f32) for r in range(FX)], axis=0
            )
            if high - low < LANES:
                end = jnp.zeros((cells, LANES - (high - low)), f32)
                block = jnp.concatenate([block, end], axis=1)
            blocks.append(block)
        turned[n * LANES : (n + 1) * LANES, :] = jnp.concatenate(blocks, axis=0).T
    for n in range(columns // per):
        rows = [turned[pl.ds(n * per + k, LANES // per, stride=columns), :] for k in range(per)]
        block = jnp.concatenate(rows, axis=0).T
        for k in range(per):
            lanes = slice(k * (LANES // per), (k + 1) * (LANES // per))
            flat[pl.ds(n * per + k, cells, stride=columns), :] = jnp.concatenate(
                [block[q * cells : (q + 1) * cells, lanes] for q in range(parts)], axis=1
            )


def dofs_first(flat, turned, out_ref):
    cells, columns = FX * FY, flat.shape[0] // (FX * FY)
    length = out_ref.shape[2]
    per = LANES // columns
    parts = LANES // cells
    steps = LANES // (per * parts)
    span = LANES // parts
    for n in range(columns // per):
        rows = [flat[pl.ds(n * per + k, cells, stride=columns), :] for k in range(per)]
        block = jnp.concatenate(
            [
                jnp.concatenate([row[:, q * span : (q + 1) * span] for row in rows], axis=1)
                for q in range(parts)
            ],
            axis=0,
        ).T
        for k in range(per):
            turned[pl.ds(n * per + k, LANES // per, stride=columns), :] = block[
                k * (LANES // per) : (k + 1) * (LANES // per)
            ]
    for n in range(steps):
        block = turned[n * LANES : (n + 1) * LANES, :].T
        for q in range(parts):
            low = (q * steps + n) * LANES
            high = min(low + LANES, length)
            for r in range(FX):
                top = q * cells + r * FY
                out_ref[r, :, low:high] = block[top : top + FY, : high - low].astype(out_ref.dtype)


def kernel(
    subs, slabs, slots, dofs,
    basis_ref, jac_hbm, faces_ref, kinds_ref, count_ref, ids_ref,
    out_ref, coarse_ref,
    x_ref, turned, flat, field, lists, meta_ref, raw, jac, stacked, pieces, running, totals, sent, sent_cols, sent_diag, sent_cols_2,
    rim_cols, got_rows, got_cols, got_diag, got_rows_2, got_cols_2,
    one_hot, row_hot, dense, got_dense, row_sum, got_sum,
    list_sem, jac_sem, s0, r0, s1, r1, s2, r2, cs1, cr1, cs2, cr2,
):
    i = lax.axis_index("sub")
    j = lax.axis_index("slab")
    up, down, left, right = i > 0, i < subs - 1, j > 0, j < slabs - 1
    columns = x_ref.shape[1]
    f32 = jnp.float32
    bf16 = jnp.bfloat16

    jac_copies = [
        pltpu.make_async_copy(
            jac_hbm.at[pl.ds(p * dofs, dofs)], raw.at[pl.ds(p * dofs, dofs)], jac_sem.at[p]
        )
        for p in range(6)
    ]
    for copy in jac_copies:
        copy.start()

    barrier = pltpu.get_barrier_semaphore()

    def greet(di, dj):
        pl.semaphore_signal(barrier, inc=1, device_id={"sub": di, "slab": dj}, device_id_type=MESH)

    diagonals = (
        (jnp.logical_and(down, right), i + 1, j + 1),
        (jnp.logical_and(down, left), i + 1, j - 1),
        (jnp.logical_and(up, right), i - 1, j + 1),
        (jnp.logical_and(up, left), i - 1, j - 1),
    )
    from_diagonals = tuple(diagonals[3 - k][0] for k in range(4))

    @pl.loop(1, subs)
    def _(k):
        greet(lax.rem(i + k, subs), j)

    @pl.loop(1, slabs)
    def _(k):
        greet(i, lax.rem(j + k, slabs))

    for there, di, dj in diagonals:
        @pl.when(there)
        def _():
            greet(di, dj)

    index_lists(faces_ref, kinds_ref, count_ref[0], lists)
    list_copy = pltpu.make_async_copy(lists, meta_ref, list_sem)
    list_copy.start()

    ids = jnp.concatenate([ids_ref[...]] * 2, axis=1)
    spots = lax.broadcasted_iota(jnp.int32, one_hot.shape, 0)
    one_hot[...] = jnp.where(spots == ids, 1.0, 0.0).astype(bf16)
    rows = lax.broadcasted_iota(jnp.int32, row_hot.shape, 0)
    spot = jnp.where(rows % 8 < CV, rows // 8 * CV + rows % 8, -1)
    row_hot[...] = jnp.where(spot == ids, 1.0, 0.0).astype(bf16)

    running[0] = jnp.zeros(running.shape[1:], f32)
    for k in range(GROUP):
        stacked[slots + k] = jnp.zeros(stacked.shape[1:], bf16)
    blank = jnp.zeros((columns, LANES), bf16)
    for c in (cell(0, 0), cell(0, EY - 1), cell(EX - 1, 0), cell(EX - 1, EY - 1)):
        field[c] = blank

    def fill(there, ref):
        @pl.when(jnp.logical_not(there))
        def _():
            ref[...] = jnp.zeros(ref.shape, ref.dtype)

    sides = (up, down, left, right)
    fill(up, field.at[pl.ds(cell(0, 1), FY)])
    fill(down, field.at[pl.ds(cell(EX - 1, 1), FY)])
    fill(left, rim_cols.at[0])
    fill(right, rim_cols.at[1])
    fill(up, got_rows.at[0])
    fill(down, got_rows.at[1])
    fill(left, got_cols.at[0])
    fill(right, got_cols.at[1])
    fill(up, got_rows_2.at[0])
    fill(down, got_rows_2.at[1])
    fill(left, got_cols_2.at[0])
    fill(right, got_cols_2.at[1])
    for k in range(4):
        fill(from_diagonals[k], got_diag.at[k])

    columns_first(basis_ref, turned, flat)
    for r in range(FX):
        for c in range(FY):
            k = r * FY + c
            block = flat[k * columns : (k + 1) * columns, :].astype(bf16)
            x_ref[k] = block
            field[cell(r + 1, c + 1)] = block

    vertical = up.astype(jnp.int32) + down.astype(jnp.int32)
    sideways = left.astype(jnp.int32) + right.astype(jnp.int32)
    pl.semaphore_wait(barrier, subs - 1 + slabs - 1 + vertical * sideways)

    def remote(src, dst, send, recv, di, dj):
        return pltpu.make_async_remote_copy(
            src_ref=src, dst_ref=dst, send_sem=send, recv_sem=recv,
            device_id={"sub": di, "slab": dj}, device_id_type=MESH,
        )

    def exchange(copies):
        for there, coming, copy in copies:
            @pl.when(there)
            def _():
                copy.start()

    def arrive(copies):
        for there, coming, copy in copies:
            @pl.when(coming)
            def _():
                copy.wait_recv()

    def leave(copies):
        for there, coming, copy in copies:
            @pl.when(there)
            def _():
                copy.wait_send()

    x_cols = x_ref.reshape(FX, FY, columns, LANES)
    first = (
        (up, down, remote(x_ref.at[pl.ds(0, FY)], field.at[pl.ds(cell(EX - 1, 1), FY)],
                          s0.at[0], r0.at[0], i - 1, j)),
        (down, up, remote(x_ref.at[pl.ds((FX - 1) * FY, FY)], field.at[pl.ds(cell(0, 1), FY)],
                          s0.at[1], r0.at[1], i + 1, j)),
        (left, right, remote(x_cols.at[:, 0], rim_cols.at[1], s0.at[2], r0.at[2], i, j - 1)),
        (right, left, remote(x_cols.at[:, FY - 1], rim_cols.at[0], s0.at[3], r0.at[3], i, j + 1)),
    )
    exchange(first)

    for copy in jac_copies:
        copy.wait()

    @pl.loop(0, 6)
    def _(r):
        top = pl.multiple_of(r * LANES, LANES)
        for t in range(TYPES):
            face_rows = raw[pl.ds(r * dofs, dofs), t, :]
            end = jnp.zeros((dofs, LANES - dofs), bf16)
            for p in range(6):
                lanes = slice(p * LANES, (p + 1) * LANES)
                jac[t, pl.ds(top + LANES - 16, 16), lanes] = jnp.zeros((16, LANES), bf16)
                jac[t, pl.ds(top, dofs), lanes] = jnp.concatenate(
                    [face_rows[:, p * dofs : (p + 1) * dofs], end], axis=1
                )

    list_copy.wait()
    arrive(first)
    for r in range(FX):
        field[cell(r + 1, 0)] = rim_cols[0, r]
        field[cell(r + 1, EY - 1)] = rim_cols[1, r]

    rows_in = columns * GROUP
    groups = group_count(slots)

    def apply():
        @pl.loop(0, slots // GATHER)
        def _(g):
            for k in range(GATHER):
                e = g * GATHER + k
                for p in range(6):
                    stacked[e, :, p * LANES : (p + 1) * LANES] = field[meta_ref[e, 3 + p]]

        @pl.loop(0, groups // TOGETHER)
        def _(n):
            for m in range(TOGETHER):
                g = n * TOGETHER + m
                x = stacked[pl.ds(meta_ref[g, 10], GROUP)].reshape(rows_in, 6 * LANES)
                y = lax.dot_general(x, jac[meta_ref[g, 9]], NT, preferred_element_type=f32)
                for k in range(GROUP):
                    for p in range(6):
                        pieces[(g * GROUP + k) * 6 + p] = y[
                            k * columns : (k + 1) * columns, p * LANES : (p + 1) * LANES
                        ]

        def add(n, total):
            for k in range(SUMS):
                at = n * SUMS + k
                total = jnp.where(meta_ref[at, 1] > 0, 0.0, total) + pieces[meta_ref[at, 0]]
                running[1 + at] = total
            return total

        lax.fori_loop(0, 6 * slots // SUMS, add, jnp.zeros((columns, LANES), f32))

        @pl.loop(0, CELLS // SPREAD)
        def _(n):
            for k in range(SPREAD):
                c = n * SPREAD + k
                total = running[meta_ref[c, 2]]
                totals[c] = total
                sent[c] = total.astype(bf16)

    apply()
    for r in range(FX):
        for k in range(2):
            sent_cols[0, r, k] = sent[cell(r + 1, k)]
            sent_cols[1, r, k] = sent[cell(r + 1, FY + k)]
    corners = (
        (cell(FX, EY - 1), cell(EX - 1, FY)),
        (cell(FX, 0), cell(EX - 1, 1)),
        (cell(1, EY - 1), cell(0, FY)),
        (cell(1, 0), cell(0, 1)),
    )
    for k in range(4):
        for n in range(2):
            sent_diag[k, n] = sent[corners[k][n]]
    span = EY + FY
    second = (
        (up, down, remote(sent.at[pl.ds(cell(0, 1), span)], got_rows.at[1],
                          s1.at[0], r1.at[0], i - 1, j)),
        (down, up, remote(sent.at[pl.ds(cell(FX, 1), span)], got_rows.at[0],
                          s1.at[1], r1.at[1], i + 1, j)),
        (left, right, remote(sent_cols.at[0], got_cols.at[1], s1.at[2], r1.at[2], i, j - 1)),
        (right, left, remote(sent_cols.at[1], got_cols.at[0], s1.at[3], r1.at[3], i, j + 1)),
    ) + tuple(
        (diagonals[k][0], from_diagonals[k],
         remote(sent_diag.at[k], got_diag.at[k], s1.at[4 + k], r1.at[4 + k],
                diagonals[k][1], diagonals[k][2]))
        for k in range(4)
    )
    exchange(second)
    leave(first)
    arrive(second)

    def wide(ref, *at):
        return ref[at].astype(f32)

    for r in range(1, FX + 1):
        for c in range(1, FY + 1):
            v = totals[cell(r, c)]
            if r == 1:
                v = v + wide(got_rows, 0, EY + c - 1)
            if r == FX:
                v = v + wide(got_rows, 1, c - 1)
            if c == 1:
                v = v + wide(got_cols, 0, r - 1, 1)
            if c == FY:
                v = v + wide(got_cols, 1, r - 1, 0)
            field[cell(r, c)] = v.astype(bf16)

    def keep(there, c, v):
        field[c] = jnp.where(there, v, 0.0).astype(bf16)

    for c in range(1, FY + 1):
        v = totals[cell(0, c)] + wide(got_rows, 0, c - 1)
        w = totals[cell(EX - 1, c)] + wide(got_rows, 1, EY + c - 1)
        if c == 1:
            v, w = v + wide(got_diag, 0, 0), w + wide(got_diag, 2, 0)
        if c == FY:
            v, w = v + wide(got_diag, 1, 0), w + wide(got_diag, 3, 0)
        keep(up, cell(0, c), v)
        keep(down, cell(EX - 1, c), w)
    for r in range(1, FX + 1):
        v = totals[cell(r, 0)] + wide(got_cols, 0, r - 1, 0)
        w = totals[cell(r, EY - 1)] + wide(got_cols, 1, r - 1, 1)
        if r == 1:
            v, w = v + wide(got_diag, 0, 1), w + wide(got_diag, 1, 1)
        if r == FX:
            v, w = v + wide(got_diag, 2, 1), w + wide(got_diag, 3, 1)
        keep(left, cell(r, 0), v)
        keep(right, cell(r, EY - 1), w)

    own = range(FX * FY)
    local = lax.dot_general(
        jnp.concatenate([x_ref[k] for k in own], axis=1),
        jnp.concatenate([field[cell(k // FY + 1, k % FY + 1)] for k in own], axis=1),
        NT, preferred_element_type=f32,
    )
    local = local * (1.0 / math.sqrt(FX * FY * dofs))
    placed = lax.dot_general(
        two_parts(local, 1), one_hot[...], NT, preferred_element_type=f32
    )
    dense[...] = jnp.dot(row_hot[...], two_parts(placed, 0), preferred_element_type=f32)

    def block(s):
        return dense.at[pl.ds(pl.multiple_of(s * 8, 8), 8)]

    def to_sub(s):
        return remote(block(s), got_dense.at[i], cs1.at[s], cr1.at[i], s, j)

    def from_sub(s):
        return remote(block(s), got_dense.at[s], cs1.at[s], cr1.at[s], s, j)

    def to_slab(s):
        return remote(row_sum, got_sum.at[j], cs2.at[s], cr2.at[j], i, s)

    def from_slab(s):
        return remote(row_sum, got_sum.at[s], cs2.at[s], cr2.at[s], i, s)

    @pl.loop(1, subs)
    def _(k):
        to_sub(lax.rem(i + k, subs)).start()

    leave(second)
    apply()

    for r in range(FX):
        sent_cols_2[0, r] = sent[cell(r + 1, 0)]
        sent_cols_2[1, r] = sent[cell(r + 1, EY - 1)]
    third = (
        (up, down, remote(sent.at[pl.ds(cell(0, 1), FY)], got_rows_2.at[1],
                          s2.at[0], r2.at[0], i - 1, j)),
        (down, up, remote(sent.at[pl.ds(cell(EX - 1, 1), FY)], got_rows_2.at[0],
                          s2.at[1], r2.at[1], i + 1, j)),
        (left, right, remote(sent_cols_2.at[0], got_cols_2.at[1], s2.at[2], r2.at[2], i, j - 1)),
        (right, left, remote(sent_cols_2.at[1], got_cols_2.at[0], s2.at[3], r2.at[3], i, j + 1)),
    )
    exchange(third)

    row_sum[...] = block(i)[...]

    @pl.loop(1, subs)
    def _(k):
        s = lax.rem(i + k, subs)
        from_sub(s).wait_recv()
        row_sum[...] += got_dense[s]

    @pl.loop(1, slabs)
    def _(k):
        to_slab(lax.rem(j + k, slabs)).start()

    arrive(third)
    for r in range(1, FX + 1):
        for c in range(1, FY + 1):
            v = totals[cell(r, c)]
            if r == 1:
                v = v + wide(got_rows_2, 0, c - 1)
            if r == FX:
                v = v + wide(got_rows_2, 1, c - 1)
            if c == 1:
                v = v + wide(got_cols_2, 0, r - 1)
            if c == FY:
                v = v + wide(got_cols_2, 1, r - 1)
            top = ((r - 1) * FY + c - 1) * columns
            flat[top : top + columns, :] = v
    dofs_first(flat, turned, out_ref)

    coarse_ref[...] = row_sum[...]

    @pl.loop(1, slabs)
    def _(k):
        s = lax.rem(j + k, slabs)
        from_slab(s).wait_recv()
        coarse_ref[...] += got_sum[s]

    leave(third)

    @pl.loop(1, subs)
    def _(k):
        to_sub(lax.rem(i + k, subs)).wait_send()

    @pl.loop(1, slabs)
    def _(k):
        to_slab(lax.rem(j + k, slabs)).wait_send()


def body(coarse_basis, jacobians, element_faces, element_type, element_count, vertex_ids):
    subs, slabs = lax.axis_size("sub"), lax.axis_size("slab")
    dofs = jacobians.shape[1] // 6
    columns = coarse_basis.shape[2] // dofs
    slots = element_faces.shape[0]
    vertex_total = CV * subs
    width = -(-vertex_total // LANES) * LANES
    f32, bf16 = jnp.float32, jnp.bfloat16

    groups = group_count(slots)
    jac = jacobians.transpose(1, 0, 2)

    def block(*lead):
        return pltpu.VMEM((*lead, columns, LANES), bf16)

    vmem = pl.BlockSpec(memory_space=pltpu.VMEM)
    dma = pltpu.SemaphoreType.DMA
    out, coarse = pl.pallas_call(
        functools.partial(kernel, subs, slabs, slots, dofs),
        out_shape=(
            jax.ShapeDtypeStruct(coarse_basis.shape, bf16),
            jax.ShapeDtypeStruct((8, width), f32),
        ),
        in_specs=[
            vmem,
            pl.BlockSpec(memory_space=pl.ANY),
            vmem,
            vmem,
            pl.BlockSpec(memory_space=pltpu.SMEM),
            vmem,
        ],
        out_specs=(vmem, vmem),
        scratch_shapes=[
            block(FX * FY),
            pltpu.VMEM((columns * LANES // (LANES // (FX * FY)), LANES), f32),
            pltpu.VMEM((FX * FY * columns, LANES), f32),
            block(CELLS),
            pltpu.VMEM((6 * slots, LANES), jnp.int32),
            pltpu.SMEM((6 * slots, LANES), jnp.int32),
            pltpu.VMEM((6 * dofs, TYPES, 6 * dofs), bf16),
            pltpu.VMEM((TYPES, 6 * LANES, 6 * LANES), bf16),
            pltpu.VMEM((slots + GROUP, columns, 6 * LANES), bf16),
            pltpu.VMEM((6 * GROUP * groups, columns, LANES), f32),
            pltpu.VMEM((1 + 6 * slots, columns, LANES), f32),
            pltpu.VMEM((CELLS, columns, LANES), f32),
            block(CELLS),
            block(2, FX, 2),
            block(4, 2),
            block(2, FX),
            block(2, FX),
            block(2, EY + FY),
            block(2, FX, 2),
            block(4, 2),
            block(2, FY),
            block(2, FX),
            pltpu.VMEM((width, 2 * columns), bf16),
            pltpu.VMEM((8 * subs, 2 * columns), bf16),
            pltpu.VMEM((8 * subs, width), f32),
            pltpu.VMEM((subs, 8, width), f32),
            pltpu.VMEM((8, width), f32),
            pltpu.VMEM((slabs, 8, width), f32),
            dma, dma((6,)),
            dma((4,)), dma((4,)),
            dma((8,)), dma((8,)),
            dma((4,)), dma((4,)),
            dma((subs,)), dma((subs,)),
            dma((slabs,)), dma((slabs,)),
        ],
        compiler_params=pltpu.CompilerParams(
            collective_id=0, has_side_effects=True, vmem_limit_bytes=40 * 1024 * 1024
        ),
        cost_estimate=pl.CostEstimate(
            flops=4 * slots * (6 * dofs) ** 2 * columns,
            bytes_accessed=2 * jacobians.size,
            transcendentals=0,
        ),
    )(coarse_basis, jac, element_faces.T, element_type.reshape(1, slots), element_count, vertex_ids)
    return out, coarse[:CV, :vertex_total]


def solution(mesh):
    return jax.shard_map(
        body,
        mesh=mesh,
        in_specs=(
            P("sub", "slab", None),
            P(),
            P(("sub", "slab"), None),
            P(("sub", "slab")),
            P(("sub", "slab")),
            P(("sub", "slab"), None),
        ),
        out_specs=(P("sub", "slab", None), P("sub", None)),
        check_vma=False,
    )
```

```python
import functools
import math

import jax
import jax.numpy as jnp
from jax import lax
from jax.experimental import pallas as pl
from jax.experimental.pallas import tpu as pltpu
from jax.sharding import PartitionSpec as P

FX = 4
FY = 8
EX = FX + 2
EY = FY + 2
CELLS = EX * EY
CV = 4
TYPES = 4
LANES = 128
GROUP = 4
GATHER = 10
TOGETHER = 4
SUMS = 20
SPREAD = 10
MESH = pl.DeviceIdType.MESH
NT = (((1,), (1,)), ((), ()))


def cell(r, c):
    return r * EY + c


def group_count(slots):
    return (slots + TYPES * (GROUP - 1)) // GROUP


def index_lists(faces_ref, kinds_ref, count, lists):
    slots, groups = faces_ref.shape[1], group_count(faces_ref.shape[1])
    i32 = jnp.int32

    def iota(rows, cols, axis):
        return lax.broadcasted_iota(i32, (rows, cols), axis)

    def count_of(mask, axis):
        return jnp.sum(jnp.where(mask, 1, 0), axis=axis, keepdims=True)

    def as_column(row):
        n = row.shape[1]
        return jnp.sum(jnp.where(iota(n, n, 0) == iota(n, n, 1), row, 0), axis=1, keepdims=True)

    def put(lane, column):
        lists[pl.ds(0, column.shape[0]), lane : lane + 1] = column

    lists[...] = jnp.zeros(lists.shape, i32)
    live = iota(1, slots, 1) < count
    kind = jnp.where(live, kinds_ref[...], TYPES)
    kind_col = as_column(kind)
    earlier = iota(slots, slots, 0) < iota(slots, slots, 1)
    in_kind = count_of((kind_col == kind) & earlier, 0)
    place = in_kind + count_of(kind_col < kind, 0)
    group = iota(groups, 1, 0)
    group_type = jnp.zeros((groups, 1), i32)
    group_start = jnp.zeros((groups, 1), i32)
    position = in_kind
    first_group = jnp.zeros((1, 1), i32)
    first_place = jnp.zeros((1, 1), i32)
    for t in range(TYPES):
        number = count_of(kind == t, 1)
        needed = lax.shift_right_logical(number + (GROUP - 1), 2)
        inside = (group >= first_group) & (group < first_group + needed)
        group_type = jnp.where(inside, t, group_type)
        group_start = jnp.where(inside, first_place + GROUP * (group - first_group), group_start)
        position = position + jnp.where(kind == t, GROUP * first_group, 0)
        first_group = first_group + needed
        first_place = first_place + number
    faces = [faces_ref[p : p + 1, :] for p in range(6)]
    cells = jnp.concatenate([jnp.where(live, f, CELLS) for f in faces], axis=1)
    piece = jnp.concatenate([position * 6 + p for p in range(6)], axis=1)
    total = 6 * slots
    cells_col = as_column(cells)
    before = iota(total, total, 0) < iota(total, total, 1)
    in_cell = count_of((cells_col == cells) & before, 0)
    rank = in_cell + count_of(cells_col < cells, 0)
    chosen = rank == iota(total, 1, 0)
    put(0, jnp.sum(jnp.where(chosen, piece, 0), axis=1, keepdims=True))
    put(1, jnp.sum(jnp.where(chosen, jnp.where(in_cell == 0, 1, 0), 0), axis=1, keepdims=True))
    spot = iota(CELLS, 1, 0)
    upto = count_of(cells <= spot, 1)
    put(2, jnp.where(count_of(cells == spot, 1) > 0, upto, 0))
    taken = place == iota(slots, 1, 0)
    for p in range(6):
        put(3 + p, jnp.sum(jnp.where(taken, faces[p], 0), axis=1, keepdims=True))
    put(9, group_type)
    put(10, group_start)


def two_parts(x, axis):
    high = x.astype(jnp.bfloat16)
    rest = (x - high.astype(jnp.float32)).astype(jnp.bfloat16)
    return jnp.concatenate([high, rest], axis=axis)


def columns_first(basis_ref, turned, flat):
    f32 = jnp.float32
    cells, columns = FX * FY, flat.shape[0] // (FX * FY)
    length = basis_ref.shape[2]
    per = LANES // columns
    parts = LANES // cells
    steps = LANES // (per * parts)
    for n in range(steps):
        blocks = []
        for q in range(parts):
            low = (q * steps + n) * LANES
            high = min(low + LANES, length)
            block = jnp.concatenate(
                [basis_ref[r, :, low:high].astype(f32) for r in range(FX)], axis=0
            )
            if high - low < LANES:
                end = jnp.zeros((cells, LANES - (high - low)), f32)
                block = jnp.concatenate([block, end], axis=1)
            blocks.append(block)
        turned[n * LANES : (n + 1) * LANES, :] = jnp.concatenate(blocks, axis=0).T
    for n in range(columns // per):
        rows = [turned[pl.ds(n * per + k, LANES // per, stride=columns), :] for k in range(per)]
        block = jnp.concatenate(rows, axis=0).T
        for k in range(per):
            lanes = slice(k * (LANES // per), (k + 1) * (LANES // per))
            flat[pl.ds(n * per + k, cells, stride=columns), :] = jnp.concatenate(
                [block[q * cells : (q + 1) * cells, lanes] for q in range(parts)], axis=1
            )


def dofs_first(flat, turned, out_ref):
    cells, columns = FX * FY, flat.shape[0] // (FX * FY)
    length = out_ref.shape[2]
    per = LANES // columns
    parts = LANES // cells
    steps = LANES // (per * parts)
    span = LANES // parts
    for n in range(columns // per):
        rows = [flat[pl.ds(n * per + k, cells, stride=columns), :] for k in range(per)]
        block = jnp.concatenate(
            [
                jnp.concatenate([row[:, q * span : (q + 1) * span] for row in rows], axis=1)
                for q in range(parts)
            ],
            axis=0,
        ).T
        for k in range(per):
            turned[pl.ds(n * per + k, LANES // per, stride=columns), :] = block[
                k * (LANES // per) : (k + 1) * (LANES // per)
            ]
    for n in range(steps):
        block = turned[n * LANES : (n + 1) * LANES, :].T
        for q in range(parts):
            low = (q * steps + n) * LANES
            high = min(low + LANES, length)
            for r in range(FX):
                top = q * cells + r * FY
                out_ref[r, :, low:high] = block[top : top + FY, : high - low].astype(out_ref.dtype)


def kernel(
    subs, slabs, slots, dofs,
    basis_ref, jac_ref, faces_ref, kinds_ref, count_ref, ids_ref,
    out_ref, coarse_ref,
    x_ref, turned, flat, field, lists, meta_ref, jac, stacked, pieces, running, totals, sent, sent_cols, sent_diag, sent_cols_2,
    rim_cols, got_rows, got_cols, got_diag, got_rows_2, got_cols_2,
    one_hot, row_hot, dense, got_dense, row_sum, got_sum,
    list_sem, s0, r0, s1, r1, s2, r2, cs1, cr1, cs2, cr2,
):
    i = lax.axis_index("sub")
    j = lax.axis_index("slab")
    up, down, left, right = i > 0, i < subs - 1, j > 0, j < slabs - 1
    columns = x_ref.shape[1]
    f32 = jnp.float32
    bf16 = jnp.bfloat16

    barrier = pltpu.get_barrier_semaphore()

    def greet(di, dj):
        pl.semaphore_signal(barrier, inc=1, device_id={"sub": di, "slab": dj}, device_id_type=MESH)

    diagonals = (
        (jnp.logical_and(down, right), i + 1, j + 1),
        (jnp.logical_and(down, left), i + 1, j - 1),
        (jnp.logical_and(up, right), i - 1, j + 1),
        (jnp.logical_and(up, left), i - 1, j - 1),
    )
    from_diagonals = tuple(diagonals[3 - k][0] for k in range(4))

    @pl.loop(1, subs)
    def _(k):
        greet(lax.rem(i + k, subs), j)

    @pl.loop(1, slabs)
    def _(k):
        greet(i, lax.rem(j + k, slabs))

    for there, di, dj in diagonals:
        @pl.when(there)
        def _():
            greet(di, dj)

    ids = jnp.concatenate([ids_ref[...]] * 2, axis=1)
    spots = lax.broadcasted_iota(jnp.int32, one_hot.shape, 0)
    one_hot[...] = jnp.where(spots == ids, 1.0, 0.0).astype(bf16)
    rows = lax.broadcasted_iota(jnp.int32, row_hot.shape, 0)
    spot = jnp.where(rows % 8 < CV, rows // 8 * CV + rows % 8, -1)
    row_hot[...] = jnp.where(spot == ids, 1.0, 0.0).astype(bf16)

    running[0] = jnp.zeros(running.shape[1:], f32)
    for k in range(GROUP):
        stacked[slots + k] = jnp.zeros(stacked.shape[1:], bf16)
    blank = jnp.zeros((columns, LANES), bf16)
    for c in (cell(0, 0), cell(0, EY - 1), cell(EX - 1, 0), cell(EX - 1, EY - 1)):
        field[c] = blank

    def fill(there, ref):
        @pl.when(jnp.logical_not(there))
        def _():
            ref[...] = jnp.zeros(ref.shape, ref.dtype)

    sides = (up, down, left, right)
    fill(up, field.at[pl.ds(cell(0, 1), FY)])
    fill(down, field.at[pl.ds(cell(EX - 1, 1), FY)])
    fill(left, rim_cols.at[0])
    fill(right, rim_cols.at[1])
    fill(up, got_rows.at[0])
    fill(down, got_rows.at[1])
    fill(left, got_cols.at[0])
    fill(right, got_cols.at[1])
    fill(up, got_rows_2.at[0])
    fill(down, got_rows_2.at[1])
    fill(left, got_cols_2.at[0])
    fill(right, got_cols_2.at[1])
    for k in range(4):
        fill(from_diagonals[k], got_diag.at[k])

    columns_first(basis_ref, turned, flat)
    for r in range(FX):
        for c in range(FY):
            k = r * FY + c
            block = flat[k * columns : (k + 1) * columns, :].astype(bf16)
            x_ref[k] = block
            field[cell(r + 1, c + 1)] = block

    vertical = up.astype(jnp.int32) + down.astype(jnp.int32)
    sideways = left.astype(jnp.int32) + right.astype(jnp.int32)
    pl.semaphore_wait(barrier, subs - 1 + slabs - 1 + vertical * sideways)

    def remote(src, dst, send, recv, di, dj):
        return pltpu.make_async_remote_copy(
            src_ref=src, dst_ref=dst, send_sem=send, recv_sem=recv,
            device_id={"sub": di, "slab": dj}, device_id_type=MESH,
        )

    def exchange(copies):
        for there, coming, copy in copies:
            @pl.when(there)
            def _():
                copy.start()

    def arrive(copies):
        for there, coming, copy in copies:
            @pl.when(coming)
            def _():
                copy.wait_recv()

    def leave(copies):
        for there, coming, copy in copies:
            @pl.when(there)
            def _():
                copy.wait_send()

    x_cols = x_ref.reshape(FX, FY, columns, LANES)
    first = (
        (up, down, remote(x_ref.at[pl.ds(0, FY)], field.at[pl.ds(cell(EX - 1, 1), FY)],
                          s0.at[0], r0.at[0], i - 1, j)),
        (down, up, remote(x_ref.at[pl.ds((FX - 1) * FY, FY)], field.at[pl.ds(cell(0, 1), FY)],
                          s0.at[1], r0.at[1], i + 1, j)),
        (left, right, remote(x_cols.at[:, 0], rim_cols.at[1], s0.at[2], r0.at[2], i, j - 1)),
        (right, left, remote(x_cols.at[:, FY - 1], rim_cols.at[0], s0.at[3], r0.at[3], i, j + 1)),
    )
    exchange(first)
    index_lists(faces_ref, kinds_ref, count_ref[0], lists)
    list_copy = pltpu.make_async_copy(lists, meta_ref, list_sem)
    list_copy.start()


    @pl.loop(0, TYPES * 6)
    def _(n):
        t, r = n // 6, n % 6
        top = pl.multiple_of(r * LANES, LANES)
        face_rows = jac_ref[t, r]
        end = jnp.zeros((dofs, LANES - dofs), bf16)
        for p in range(6):
            lanes = slice(p * LANES, (p + 1) * LANES)
            jac[t, pl.ds(top + LANES - 16, 16), lanes] = jnp.zeros((16, LANES), bf16)
            jac[t, pl.ds(top, dofs), lanes] = jnp.concatenate(
                [face_rows[:, p * dofs : (p + 1) * dofs], end], axis=1
            )

    list_copy.wait()
    arrive(first)
    for r in range(FX):
        field[cell(r + 1, 0)] = rim_cols[0, r]
        field[cell(r + 1, EY - 1)] = rim_cols[1, r]

    rows_in = columns * GROUP
    groups = group_count(slots)

    def apply():
        @pl.loop(0, slots // GATHER)
        def _(g):
            for k in range(GATHER):
                e = g * GATHER + k
                for p in range(6):
                    stacked[e, :, p * LANES : (p + 1) * LANES] = field[meta_ref[e, 3 + p]]

        @pl.loop(0, groups // TOGETHER)
        def _(n):
            for m in range(TOGETHER):
                g = n * TOGETHER + m
                x = stacked[pl.ds(meta_ref[g, 10], GROUP)].reshape(rows_in, 6 * LANES)
                y = lax.dot_general(x, jac[meta_ref[g, 9]], NT, preferred_element_type=f32)
                for k in range(GROUP):
                    for p in range(6):
                        pieces[(g * GROUP + k) * 6 + p] = y[
                            k * columns : (k + 1) * columns, p * LANES : (p + 1) * LANES
                        ]

        def add(n, total):
            for k in range(SUMS):
                at = n * SUMS + k
                total = jnp.where(meta_ref[at, 1] > 0, 0.0, total) + pieces[meta_ref[at, 0]]
                running[1 + at] = total
            return total

        lax.fori_loop(0, 6 * slots // SUMS, add, jnp.zeros((columns, LANES), f32))

        @pl.loop(0, CELLS // SPREAD)
        def _(n):
            for k in range(SPREAD):
                c = n * SPREAD + k
                total = running[meta_ref[c, 2]]
                totals[c] = total
                sent[c] = total.astype(bf16)

    apply()
    for r in range(FX):
        for k in range(2):
            sent_cols[0, r, k] = sent[cell(r + 1, k)]
            sent_cols[1, r, k] = sent[cell(r + 1, FY + k)]
    corners = (
        (cell(FX, EY - 1), cell(EX - 1, FY)),
        (cell(FX, 0), cell(EX - 1, 1)),
        (cell(1, EY - 1), cell(0, FY)),
        (cell(1, 0), cell(0, 1)),
    )
    for k in range(4):
        for n in range(2):
            sent_diag[k, n] = sent[corners[k][n]]
    span = EY + FY
    second = (
        (up, down, remote(sent.at[pl.ds(cell(0, 1), span)], got_rows.at[1],
                          s1.at[0], r1.at[0], i - 1, j)),
        (down, up, remote(sent.at[pl.ds(cell(FX, 1), span)], got_rows.at[0],
                          s1.at[1], r1.at[1], i + 1, j)),
        (left, right, remote(sent_cols.at[0], got_cols.at[1], s1.at[2], r1.at[2], i, j - 1)),
        (right, left, remote(sent_cols.at[1], got_cols.at[0], s1.at[3], r1.at[3], i, j + 1)),
    ) + tuple(
        (diagonals[k][0], from_diagonals[k],
         remote(sent_diag.at[k], got_diag.at[k], s1.at[4 + k], r1.at[4 + k],
                diagonals[k][1], diagonals[k][2]))
        for k in range(4)
    )
    exchange(second)
    leave(first)
    arrive(second)

    def wide(ref, *at):
        return ref[at].astype(f32)

    for r in range(1, FX + 1):
        for c in range(1, FY + 1):
            v = totals[cell(r, c)]
            if r == 1:
                v = v + wide(got_rows, 0, EY + c - 1)
            if r == FX:
                v = v + wide(got_rows, 1, c - 1)
            if c == 1:
                v = v + wide(got_cols, 0, r - 1, 1)
            if c == FY:
                v = v + wide(got_cols, 1, r - 1, 0)
            field[cell(r, c)] = v.astype(bf16)

    def keep(there, c, v):
        field[c] = jnp.where(there, v, 0.0).astype(bf16)

    for c in range(1, FY + 1):
        v = totals[cell(0, c)] + wide(got_rows, 0, c - 1)
        w = totals[cell(EX - 1, c)] + wide(got_rows, 1, EY + c - 1)
        if c == 1:
            v, w = v + wide(got_diag, 0, 0), w + wide(got_diag, 2, 0)
        if c == FY:
            v, w = v + wide(got_diag, 1, 0), w + wide(got_diag, 3, 0)
        keep(up, cell(0, c), v)
        keep(down, cell(EX - 1, c), w)
    for r in range(1, FX + 1):
        v = totals[cell(r, 0)] + wide(got_cols, 0, r - 1, 0)
        w = totals[cell(r, EY - 1)] + wide(got_cols, 1, r - 1, 1)
        if r == 1:
            v, w = v + wide(got_diag, 0, 1), w + wide(got_diag, 1, 1)
        if r == FX:
            v, w = v + wide(got_diag, 2, 1), w + wide(got_diag, 3, 1)
        keep(left, cell(r, 0), v)
        keep(right, cell(r, EY - 1), w)

    own = range(FX * FY)
    local = lax.dot_general(
        jnp.concatenate([x_ref[k] for k in own], axis=1),
        jnp.concatenate([field[cell(k // FY + 1, k % FY + 1)] for k in own], axis=1),
        NT, preferred_element_type=f32,
    )
    local = local * (1.0 / math.sqrt(FX * FY * dofs))
    placed = lax.dot_general(
        two_parts(local, 1), one_hot[...], NT, preferred_element_type=f32
    )
    dense[...] = jnp.dot(row_hot[...], two_parts(placed, 0), preferred_element_type=f32)

    def block(s):
        return dense.at[pl.ds(pl.multiple_of(s * 8, 8), 8)]

    def to_sub(s):
        return remote(block(s), got_dense.at[i], cs1.at[s], cr1.at[i], s, j)

    def from_sub(s):
        return remote(block(s), got_dense.at[s], cs1.at[s], cr1.at[s], s, j)

    def to_slab(s):
        return remote(row_sum, got_sum.at[j], cs2.at[s], cr2.at[j], i, s)

    def from_slab(s):
        return remote(row_sum, got_sum.at[s], cs2.at[s], cr2.at[s], i, s)

    @pl.loop(1, subs)
    def _(k):
        to_sub(lax.rem(i + k, subs)).start()

    leave(second)
    apply()

    for r in range(FX):
        sent_cols_2[0, r] = sent[cell(r + 1, 0)]
        sent_cols_2[1, r] = sent[cell(r + 1, EY - 1)]
    third = (
        (up, down, remote(sent.at[pl.ds(cell(0, 1), FY)], got_rows_2.at[1],
                          s2.at[0], r2.at[0], i - 1, j)),
        (down, up, remote(sent.at[pl.ds(cell(EX - 1, 1), FY)], got_rows_2.at[0],
                          s2.at[1], r2.at[1], i + 1, j)),
        (left, right, remote(sent_cols_2.at[0], got_cols_2.at[1], s2.at[2], r2.at[2], i, j - 1)),
        (right, left, remote(sent_cols_2.at[1], got_cols_2.at[0], s2.at[3], r2.at[3], i, j + 1)),
    )
    exchange(third)

    row_sum[...] = block(i)[...]

    @pl.loop(1, subs)
    def _(k):
        s = lax.rem(i + k, subs)
        from_sub(s).wait_recv()
        row_sum[...] += got_dense[s]

    @pl.loop(1, slabs)
    def _(k):
        to_slab(lax.rem(j + k, slabs)).start()

    arrive(third)
    for r in range(1, FX + 1):
        for c in range(1, FY + 1):
            v = totals[cell(r, c)]
            if r == 1:
                v = v + wide(got_rows_2, 0, c - 1)
            if r == FX:
                v = v + wide(got_rows_2, 1, c - 1)
            if c == 1:
                v = v + wide(got_cols_2, 0, r - 1)
            if c == FY:
                v = v + wide(got_cols_2, 1, r - 1)
            top = ((r - 1) * FY + c - 1) * columns
            flat[top : top + columns, :] = v
    dofs_first(flat, turned, out_ref)

    coarse_ref[...] = row_sum[...]

    @pl.loop(1, slabs)
    def _(k):
        s = lax.rem(j + k, slabs)
        from_slab(s).wait_recv()
        coarse_ref[...] += got_sum[s]

    leave(third)

    @pl.loop(1, subs)
    def _(k):
        to_sub(lax.rem(i + k, subs)).wait_send()

    @pl.loop(1, slabs)
    def _(k):
        to_slab(lax.rem(j + k, slabs)).wait_send()


def body(coarse_basis, jacobians, element_faces, element_type, element_count, vertex_ids):
    subs, slabs = lax.axis_size("sub"), lax.axis_size("slab")
    dofs = jacobians.shape[1] // 6
    columns = coarse_basis.shape[2] // dofs
    slots = element_faces.shape[0]
    vertex_total = CV * subs
    width = -(-vertex_total // LANES) * LANES
    f32, bf16 = jnp.float32, jnp.bfloat16

    groups = group_count(slots)
    jac = jacobians.reshape(TYPES, 6, dofs, 6 * dofs)

    def block(*lead):
        return pltpu.VMEM((*lead, columns, LANES), bf16)

    vmem = pl.BlockSpec(memory_space=pltpu.VMEM)
    dma = pltpu.SemaphoreType.DMA
    out, coarse = pl.pallas_call(
        functools.partial(kernel, subs, slabs, slots, dofs),
        out_shape=(
            jax.ShapeDtypeStruct(coarse_basis.shape, bf16),
            jax.ShapeDtypeStruct((8, width), f32),
        ),
        in_specs=[
            vmem,
            vmem,
            vmem,
            vmem,
            pl.BlockSpec(memory_space=pltpu.SMEM),
            vmem,
        ],
        out_specs=(vmem, vmem),
        scratch_shapes=[
            block(FX * FY),
            pltpu.VMEM((columns * LANES // (LANES // (FX * FY)), LANES), f32),
            pltpu.VMEM((FX * FY * columns, LANES), f32),
            block(CELLS),
            pltpu.VMEM((6 * slots, LANES), jnp.int32),
            pltpu.SMEM((6 * slots, LANES), jnp.int32),
            pltpu.VMEM((TYPES, 6 * LANES, 6 * LANES), bf16),
            pltpu.VMEM((slots + GROUP, columns, 6 * LANES), bf16),
            pltpu.VMEM((6 * GROUP * groups, columns, LANES), f32),
            pltpu.VMEM((1 + 6 * slots, columns, LANES), f32),
            pltpu.VMEM((CELLS, columns, LANES), f32),
            block(CELLS),
            block(2, FX, 2),
            block(4, 2),
            block(2, FX),
            block(2, FX),
            block(2, EY + FY),
            block(2, FX, 2),
            block(4, 2),
            block(2, FY),
            block(2, FX),
            pltpu.VMEM((width, 2 * columns), bf16),
            pltpu.VMEM((8 * subs, 2 * columns), bf16),
            pltpu.VMEM((8 * subs, width), f32),
            pltpu.VMEM((subs, 8, width), f32),
            pltpu.VMEM((8, width), f32),
            pltpu.VMEM((slabs, 8, width), f32),
            dma,
            dma((4,)), dma((4,)),
            dma((8,)), dma((8,)),
            dma((4,)), dma((4,)),
            dma((subs,)), dma((subs,)),
            dma((slabs,)), dma((slabs,)),
        ],
        compiler_params=pltpu.CompilerParams(
            collective_id=0, has_side_effects=True, vmem_limit_bytes=40 * 1024 * 1024
        ),
        cost_estimate=pl.CostEstimate(
            flops=4 * slots * (6 * dofs) ** 2 * columns,
            bytes_accessed=2 * jacobians.size,
            transcendentals=0,
        ),
    )(coarse_basis, jac, element_faces.T, element_type.reshape(1, slots), element_count, vertex_ids)
    return out, coarse[:CV, :vertex_total]


def solution(mesh):
    return jax.shard_map(
        body,
        mesh=mesh,
        in_specs=(
            P("sub", "slab", None),
            P(),
            P(("sub", "slab"), None),
            P(("sub", "slab")),
            P(("sub", "slab")),
            P(("sub", "slab"), None),
        ),
        out_specs=(P("sub", "slab", None), P("sub", None)),
        check_vma=False,
    )
```
